256 devices in a mesh: blk: 8 (over y, x_hi), ulys: 32 (over z, x_lo, core).
Axes of the slice: x: 4 (x_hi: 2, x_lo: 2; x = x_hi * 2 + x_lo), y: 4, z: 8, core: 2. Of those that a mesh axis runs over, the one named last changes fastest.
Arguments:
- mamba_input: bfloat16 [16384, 16384], P(('blk', 'ulys')), may hold values from -6 to 6
- gate_input: bfloat16 [16384, 16384], P(('blk', 'ulys')), may hold values from -6 to 6
- delta_low: bfloat16 [16384, 512], P(('blk', 'ulys')), may hold values from -12 to 12
- state_mixers: bfloat16 [16384, 32], P(('blk', 'ulys')), may hold values from -6 to 6
- conv_weight: bfloat16 [4, 16384], P(None, 'ulys'), may hold values from -3 to 3
- conv_bias: float32 [16384], P('ulys'), may hold values from -3 to 3
- delta_weight: bfloat16 [512, 16384], P(None, 'ulys'), may hold values from -0.25 to 0.25
- delta_bias: float32 [16384], P('ulys'), may hold values from -12 to -2.3
- decay_log: float32 [16, 16384], P(None, 'ulys'), may hold values from -1 to 2.7
- skip_gain: float32 [16384], P('ulys'), may hold values from 0.5 to 1.5
- queries: bfloat16 [16384, 4096], P(('blk', 'ulys')), may hold values from -4.5 to 4.5
- key_rows: bfloat16 [16384, 1024], P(('blk', 'ulys')), may hold values from -4.5 to 4.5
- value_rows: bfloat16 [16384, 1024], P(('blk', 'ulys')), may hold values from -6 to 6
- span_order: int32 [16], replicated, may hold values from 0 to 15, as said below
Outputs:
- mamba_output: bfloat16 [16384, 16384], P(('blk', 'ulys'))
- attention_output: bfloat16 [16384, 4096], P(('blk', 'ulys'))
The draws below stay inside these ranges and needn't reach their ends.
Inputs may be any that keep to these rules, and one draw needn't show every extreme that they name: `span_order`: device i of blk holds stored blocks 2i and 2i+1, whose sequence places are p and 15 - p for some p below 8, in either order; every sequence place appears once; the device holding places 0 and 15 and the device holding places 1 and 14 are 4 apart along blk.
All inputs are finite; a program needn't handle non-finite values.
Results may differ from the reference program's by a relative error of at most 0.013.
Values may be sent and summed in bfloat16 or wider, within the bound.
A program may use at most 128 MiB of HBM per device.

```python
import jax
import jax.numpy as jnp
from jax import lax

INNER = 16384
STATE = 16
DT_RANK = 512
CONV = 4
KVH = 8
HD = 128
QH = 32
SPAN = 1024
NCH = 16
SEQUENCE_TOKENS = 16384


def draw_span_order(key, part):
    pair_count = NCH // 2
    firsts = jax.random.permutation(jax.random.fold_in(key, 21), pair_count).astype(jnp.int32)
    slots = jnp.arange(pair_count, dtype=jnp.int32)
    holder_zero = jnp.sum(jnp.where(firsts == 0, slots, 0)).astype(jnp.int32)
    holder_one = jnp.sum(jnp.where(firsts == 1, slots, 0)).astype(jnp.int32)
    target = ((holder_zero + pair_count // 2) % pair_count).astype(jnp.int32)
    at_target = jnp.sum(jnp.where(slots == target, firsts, 0)).astype(jnp.int32)
    firsts = jnp.where(slots == target, 1, jnp.where(slots == holder_one, at_target, firsts)).astype(jnp.int32)
    flips = jax.random.randint(jax.random.fold_in(key, 22), (pair_count,), 0, 2).astype(jnp.int32)
    lower = jnp.where(flips == 1, NCH - 1 - firsts, firsts)
    upper = NCH - 1 - lower
    return jnp.stack([lower, upper], axis=1).reshape(NCH).astype(jnp.int32)


def draw_delta_low(key, part):
    base_key = jax.random.fold_in(key, 11)
    pick_key = jax.random.fold_in(key, 12)
    starting_rows = jax.random.normal(base_key, (SEQUENCE_TOKENS, DT_RANK), jnp.float32)
    selected_rows = jax.random.randint(pick_key, (8,), 0, SEQUENCE_TOKENS)
    token_group = jnp.any(jnp.arange(SEQUENCE_TOKENS)[:, None] == selected_rows[None, :], axis=1)
    return jnp.clip(jnp.where(token_group[:, None], 5.0 * starting_rows, starting_rows), -12.0, 12.0).astype(jnp.bfloat16)


def draw_delta_bias(key, part):
    return jax.random.uniform(key, (INNER,), jnp.float32, -11.5, -2.3)


def drawn_rows(key, col_count):
    return jnp.clip(jax.random.normal(key, (SEQUENCE_TOKENS, col_count), jnp.float32), -4.5, 4.5)


def draw_queries(key, part):
    starting_rows = drawn_rows(jax.random.fold_in(key, 1), QH * HD)
    return starting_rows.astype(jnp.bfloat16)


def draw_key_rows(key, part):
    starting_rows = drawn_rows(jax.random.fold_in(key, 2), KVH * HD)
    return starting_rows.astype(jnp.bfloat16)


def block_levels(stream_key, extent, pieces, least, top_value):
    gain = 1.0
    for dim, shards_of in pieces:
        draws = jax.random.uniform(jax.random.fold_in(jax.random.fold_in(stream_key, 6), dim), (shards_of,), jnp.float32, least / len(pieces), top_value / len(pieces))
        gain = gain * jnp.repeat(jnp.exp(draws), extent[dim] // shards_of).reshape((-1,) + (1,) * (len(extent) - 1 - dim))
    return gain


def bell_draw(own_key, dims, width, most, shards=(), kind=jnp.bfloat16):
    array = jax.random.normal(own_key, dims, jnp.float32) * width
    if len(shards) > 0:
        array = block_levels(own_key, dims, shards, -0.22, 0.18) * array
    return jnp.clip(array, min=-most, max=most).astype(kind)


def setup_inputs(seed: int = 0) -> dict:
    key_of = jax.random.split(jax.random.key(seed), 15)
    mamba_input = bell_draw(key_of[0], (SEQUENCE_TOKENS, INNER), 1.0, 6.0, ((0, 256),))
    gate_input = bell_draw(key_of[1], (SEQUENCE_TOKENS, INNER), 1.0, 6.0, ((0, 256),))
    delta_low = draw_delta_low(jax.random.fold_in(key_of[14], 71), 0)
    state_mixers = bell_draw(key_of[3], (SEQUENCE_TOKENS, 2 * STATE), 1.0, 6.0, ((0, 256),))
    conv_weight = bell_draw(key_of[4], (CONV, INNER), CONV ** -0.5, 3.0, ((1, 32),))
    conv_bias = bell_draw(key_of[5], (INNER,), 0.5, 3.0, ((0, 32),), jnp.float32)
    delta_weight = bell_draw(key_of[6], (DT_RANK, INNER), DT_RANK ** -0.5, 0.25, ((1, 32),))
    delta_bias = draw_delta_bias(jax.random.fold_in(key_of[14], 71), 0)
    decay_log = jnp.clip(-1.0 + 3.7 * jax.random.uniform(key_of[8], (STATE, INNER), jnp.float32) ** block_levels(key_of[8], (STATE, INNER), ((1, 32),), -0.2, 0.2), -1.0, 2.7)
    skip_gain = jnp.clip(0.5 + 1.0 * jax.random.uniform(key_of[9], (INNER,), jnp.float32) ** block_levels(key_of[9], (INNER,), ((0, 32),), -0.2, 0.2), 0.5, 1.5)
    queries = draw_queries(jax.random.fold_in(key_of[14], 71), 0)
    key_rows = draw_key_rows(jax.random.fold_in(key_of[14], 71), 0)
    value_rows = bell_draw(key_of[12], (SEQUENCE_TOKENS, KVH * HD), 1.0, 6.0, ((0, 256),))
    span_order = draw_span_order(jax.random.fold_in(key_of[14], 71), 0)
    return dict(mamba_input=mamba_input, gate_input=gate_input, delta_low=delta_low, state_mixers=state_mixers, conv_weight=conv_weight, conv_bias=conv_bias, delta_weight=delta_weight, delta_bias=delta_bias, decay_log=decay_log, skip_gain=skip_gain, queries=queries, key_rows=key_rows, value_rows=value_rows, span_order=span_order)


NEG_LARGE = -1.0e30


def block_holder(span_order):
    places = jnp.arange(NCH, dtype=jnp.int32)
    matches = span_order[None, :] == places[:, None]
    return jnp.sum(jnp.where(matches, places[None, :], 0), axis=1).astype(jnp.int32)


def into_sequence(stored, holder):
    blocks = stored.reshape(NCH, SPAN, stored.shape[1])
    return jnp.take(blocks, holder, axis=0).reshape(stored.shape)


def into_storage(ordered, span_order):
    blocks = ordered.reshape(NCH, SPAN, ordered.shape[1])
    return jnp.take(blocks, span_order, axis=0).reshape(ordered.shape)


def split_columns(matrix, block_count):
    return matrix.reshape(matrix.shape[0], block_count, matrix.shape[1] // block_count).transpose(1, 0, 2)


def mamba_columns(columns, low_seq, mixers_seq):
    input_cols, gate_cols, conv_cols, conv_shift, delta_cols, delta_shift, decay_cols, skip_cols = columns
    col_count = input_cols.shape[1]
    padded = jnp.concatenate([jnp.zeros((CONV - 1, col_count), jnp.float32), input_cols.astype(jnp.float32)], axis=0)
    mixed_sum = jnp.broadcast_to(conv_shift[None, :], (SEQUENCE_TOKENS, col_count))
    for offset in range(CONV):
        mixed_sum = mixed_sum + conv_cols[offset].astype(jnp.float32)[None, :] * padded[offset:offset + SEQUENCE_TOKENS]
    driven = jax.nn.silu(mixed_sum)
    delta_step = jax.nn.softplus(jnp.dot(low_seq, delta_cols, preferred_element_type=jnp.float32) + delta_shift[None, :])
    decay_rates = -jnp.exp(decay_cols)
    inject = mixers_seq[:, :STATE].astype(jnp.float32)
    readout_matrix = mixers_seq[:, STATE:].astype(jnp.float32)

    def advance(hidden, inputs):
        delta_now, driven_now, inject_now, readout_now = inputs
        hidden = jnp.exp(delta_now[None, :] * decay_rates) * hidden + (delta_now * driven_now)[None, :] * inject_now[:, None]
        return hidden, jnp.sum(readout_now[:, None] * hidden, axis=0)

    _, scanned = lax.scan(advance, jnp.zeros((STATE, col_count), jnp.float32), (delta_step, driven, inject, readout_matrix))
    ssm_out = (scanned + skip_cols[None, :] * driven).astype(jnp.bfloat16)
    return (lax.optimization_barrier(ssm_out).astype(jnp.float32) * jax.nn.silu(gate_cols.astype(jnp.float32))).astype(jnp.bfloat16)


def attention_sequence(query_seq, key_seq, value_seq):
    group_size = QH // KVH
    query_block = min(SEQUENCE_TOKENS, 1024)
    score_scale = HD ** -0.5
    key_pos = jnp.arange(SEQUENCE_TOKENS, dtype=jnp.int32)

    def one_head(head_index):
        query_head = lax.dynamic_slice_in_dim(query_seq, head_index * HD, HD, 1)
        key_head = lax.dynamic_slice_in_dim(key_seq, (head_index // group_size) * HD, HD, 1)
        value_head = lax.dynamic_slice_in_dim(value_seq, (head_index // group_size) * HD, HD, 1)

        def one_block(block_index):
            query_part = lax.dynamic_slice_in_dim(query_head, block_index * query_block, query_block, 0)
            scores = jnp.dot(query_part, key_head.T, preferred_element_type=jnp.float32) * score_scale
            query_pos = block_index * query_block + jnp.arange(query_block, dtype=jnp.int32)
            allowed = key_pos[None, :] <= query_pos[:, None]
            row_top = jnp.max(jnp.where(allowed, scores, NEG_LARGE), axis=1, keepdims=True)
            weights = jnp.where(allowed, jnp.exp(scores - row_top), 0.0)
            row_total = jnp.sum(weights, axis=1, keepdims=True)
            return jnp.dot(weights.astype(jnp.bfloat16), value_head, preferred_element_type=jnp.float32) / row_total

        return lax.map(one_block, jnp.arange(SEQUENCE_TOKENS // query_block, dtype=jnp.int32))

    heads_out = lax.map(one_head, jnp.arange(QH, dtype=jnp.int32))
    return heads_out.reshape(QH, SEQUENCE_TOKENS, HD).transpose(1, 0, 2).reshape(SEQUENCE_TOKENS, QH * HD).astype(jnp.bfloat16)


def reference(mamba_input, gate_input, delta_low, state_mixers, conv_weight, conv_bias, delta_weight, delta_bias, decay_log, skip_gain, queries, key_rows, value_rows, span_order):
    holder = block_holder(span_order)
    block_cols = min(INNER, 2048)
    block_count = INNER // block_cols
    columns = (
        split_columns(into_sequence(mamba_input, holder), block_count),
        split_columns(into_sequence(gate_input, holder), block_count),
        split_columns(conv_weight, block_count),
        conv_bias.reshape(block_count, block_cols),
        split_columns(delta_weight, block_count),
        delta_bias.reshape(block_count, block_cols),
        split_columns(decay_log, block_count),
        skip_gain.reshape(block_count, block_cols),
    )
    low_seq = into_sequence(delta_low, holder)
    mixers_seq = into_sequence(state_mixers, holder)
    gated = lax.map(lambda part_cols: mamba_columns(part_cols, low_seq, mixers_seq), columns)
    mamba_seq = gated.transpose(1, 0, 2).reshape(SEQUENCE_TOKENS, INNER)
    attention_seq = attention_sequence(into_sequence(queries, holder), into_sequence(key_rows, holder), into_sequence(value_rows, holder))
    return into_storage(mamba_seq, span_order), into_storage(attention_seq, span_order)
```

```python
import functools

import jax
import jax.numpy as jnp
from jax import lax
from jax.experimental import pallas as pl
from jax.experimental.pallas import tpu as pltpu
from jax.sharding import Mesh, PartitionSpec as P

STATE = 16
CONV = 4
HD = 128
SPAN = 1024
CHUNKS = 8
CLEN = 256
COLS = 512
TILES = COLS // 128
TB = 32
STEPS = CLEN // TB
NEG_LARGE = -1e30
LOG2E = 1.4426950408889634
VMEM_LIMIT = 56 * 2**20


def tree_sum(terms):
    while len(terms) > 1:
        terms = [a + b for a, b in zip(terms[::2], terms[1::2])] + terms[len(terms) // 2 * 2 :]
    return terms[0]


def scan_kernel(
    x_ref, prior_ref, low_ref, mix_ref, spread_ref, w_ref, convw_ref, convb_ref, bias_ref, rate_ref, skip_ref,
    y_ref, cum_ref, end_ref, sum_ref, total_ref,
    delta_s, dx_s, direct_s, splat_s, tail_s, state_s, run_s,
):
    step = pl.program_id(0)

    @pl.when(step == 0)
    def _():
        tail_s[...] = prior_ref[...]
        state_s[...] = jnp.zeros_like(state_s)
        run_s[...] = jnp.zeros_like(run_s)

    splat_s[...] = jnp.dot(mix_ref[...], spread_ref[...], preferred_element_type=jnp.float32)

    def prepare(chunk, carry):
        x = x_ref[chunk].astype(jnp.float32)
        padded = jnp.concatenate([tail_s[chunk], x], axis=0)
        mixed = convb_ref[...] + convw_ref[CONV - 1 : CONV, :] * x
        for k in range(CONV - 1):
            mixed = mixed + convw_ref[k : k + 1, :] * padded[8 - (CONV - 1) + k : 8 - (CONV - 1) + k + TB]
        tail_s[chunk] = x[TB - 8 :]
        driven = mixed * jax.nn.sigmoid(mixed)
        raw = jnp.dot(low_ref[chunk], w_ref[...], preferred_element_type=jnp.float32) + bias_ref[...]
        delta = jnp.maximum(raw, 0.0) + jnp.log1p(jnp.exp(-jnp.abs(raw)))
        dx = delta * driven
        direct = skip_ref[...] * driven
        for j in range(TILES):
            cols = slice(j * 128, (j + 1) * 128)
            rows = pl.ds(chunk, TB, stride=CHUNKS)
            delta_s.at[j][rows, :] = delta[:, cols]
            dx_s.at[j][rows, :] = dx[:, cols]
            direct_s.at[j][rows, :] = direct[:, cols]
        return carry

    lax.fori_loop(0, CHUNKS, prepare, 0)

    for j in range(TILES):
        cols = slice(j * 128, (j + 1) * 128)
        rates = [jnp.broadcast_to(rate_ref[n : n + 1, cols], (CHUNKS, 128)) for n in range(STATE)]

        def advance(t, carry):
            hidden, run = carry
            rows = pl.ds(pl.multiple_of(t * CHUNKS, CHUNKS), CHUNKS)
            delta = delta_s[j, rows, :]
            dx = dx_s[j, rows, :]
            hidden = tuple(
                jnp.exp2(delta * rates[n]) * hidden[n] + dx * splat_s[rows, n * 128 : (n + 1) * 128]
                for n in range(STATE)
            )
            terms = [
                hidden[n] * splat_s[rows, (STATE + n) * 128 : (STATE + n + 1) * 128] for n in range(STATE)
            ]
            run = run + delta
            y_ref[j, rows, :] = tree_sum(terms) + direct_s[j, rows, :]
            cum_ref[j, rows, :] = run
            return (hidden, run)

        hidden, run = lax.fori_loop(
            0, TB, advance, (tuple(state_s[j, n] for n in range(STATE)), run_s[j]), unroll=4
        )
        for n in range(STATE):
            state_s[j, n] = hidden[n]
        run_s[j] = run

    @pl.when(step == STEPS - 1)
    def _():
        for j in range(TILES):
            for n in range(STATE):
                end_ref.at[j][pl.ds(n, CHUNKS, stride=STATE), :] = state_s[j, n]
            sum_ref[j] = run_s[j]
        for j in range(TILES):
            rate = rate_ref[:, j * 128 : (j + 1) * 128]
            for b in range(2):
                state = jnp.zeros((STATE, 128), jnp.float32)
                total = jnp.zeros((1, 128), jnp.float32)
                for c in range(4 * b, 4 * b + 4):
                    here = sum_ref[j, c : c + 1, :]
                    state = jnp.exp2(rate * here) * state + end_ref[j, c * STATE : (c + 1) * STATE, :]
                    total = total + here
                total_ref[b, j, :STATE] = state
                total_ref[b, j, STATE:] = jnp.broadcast_to(total, (8, 128))


def scan_call(x, prior, low, mix, spread, w, convw, convb, bias, rate, skip):
    f32 = jnp.float32
    whole = lambda shape: pl.BlockSpec(shape, lambda i: (0,) * len(shape))
    tokens = lambda width: pl.BlockSpec((CHUNKS, TB, width), lambda i: (0, i, 0))
    rows = TB * CHUNKS
    return pl.pallas_call(
        scan_kernel,
        grid=(STEPS,),
        in_specs=[
            tokens(COLS), whole((CHUNKS, 8, COLS)), tokens(512),
            pl.BlockSpec((rows, 2 * STATE), lambda i: (i, 0)), whole((2 * STATE, 2 * STATE * 128)),
            whole((512, COLS)), whole((CONV, COLS)), whole((1, COLS)), whole((1, COLS)),
            whole((STATE, COLS)), whole((1, COLS)),
        ],
        out_specs=[
            pl.BlockSpec((TILES, rows, 128), lambda i: (0, i, 0)),
            pl.BlockSpec((TILES, rows, 128), lambda i: (0, i, 0)),
            whole((TILES, CHUNKS * STATE, 128)), whole((TILES, CHUNKS, 128)), whole((2, TILES, 24, 128)),
        ],
        out_shape=[
            jax.ShapeDtypeStruct((TILES, CLEN * CHUNKS, 128), f32),
            jax.ShapeDtypeStruct((TILES, CLEN * CHUNKS, 128), f32),
            jax.ShapeDtypeStruct((TILES, CHUNKS * STATE, 128), f32),
            jax.ShapeDtypeStruct((TILES, CHUNKS, 128), f32),
            jax.ShapeDtypeStruct((2, TILES, 24, 128), f32),
        ],
        scratch_shapes=[
            pltpu.VMEM((TILES, rows, 128), f32), pltpu.VMEM((TILES, rows, 128), f32),
            pltpu.VMEM((TILES, rows, 128), f32), pltpu.VMEM((rows, 2 * STATE * 128), f32),
            pltpu.VMEM((CHUNKS, 8, COLS), f32), pltpu.VMEM((TILES, STATE, CHUNKS, 128), f32),
            pltpu.VMEM((TILES, CHUNKS, 128), f32),
        ],
        compiler_params=pltpu.CompilerParams(vmem_limit_bytes=VMEM_LIMIT),
        cost_estimate=pl.CostEstimate(flops=100_000_000_000, bytes_accessed=16 * 2**20, transcendentals=0),
        name="scan_chunks",
    )(x, prior, low, mix, spread, w, convw, convb, bias, rate, skip)


def finish_kernel(
    info_ref, y_ref, cum_ref, mix_ref, spread_ref, gate_ref, rate_ref, end_ref, sum_ref, all_ref,
    out_ref, splat_s, start_s, enter_s, ready_s,
):
    step = pl.program_id(0)

    @pl.when(step == 0)
    def _():
        for j in range(TILES):
            rate = rate_ref[:, j * 128 : (j + 1) * 128]

            def carry_on(position, state):
                enter_s[position] = state
                block = info_ref[position]
                total = all_ref[block, j, STATE : STATE + 1, :]
                return jnp.exp2(rate * total) * state + all_ref[block, j, :STATE, :]

            lax.fori_loop(0, 2 * CHUNKS, carry_on, jnp.zeros((STATE, 128), jnp.float32))
            for b in range(2):
                state = enter_s[info_ref[2 * CHUNKS + b]]
                for c in range(4 * b, 4 * b + 4):
                    start_s[j, c * STATE : (c + 1) * STATE, :] = state
                    if c < 4 * b + 3:
                        state = (
                            jnp.exp2(rate * sum_ref[j, c : c + 1, :]) * state
                            + end_ref[j, c * STATE : (c + 1) * STATE, :]
                        )

    splat_s[...] = jnp.dot(mix_ref[...], spread_ref[...], preferred_element_type=jnp.float32)

    for j in range(TILES):
        cols = slice(j * 128, (j + 1) * 128)
        rates = [jnp.broadcast_to(rate_ref[n : n + 1, cols], (CHUNKS, 128)) for n in range(STATE)]
        starts = [start_s.at[j][pl.ds(n, CHUNKS, stride=STATE), :] for n in range(STATE)]

        def correct(t, carry):
            rows = pl.ds(pl.multiple_of(t * CHUNKS, CHUNKS), CHUNKS)
            run = cum_ref[j, rows, :]
            terms = [
                jnp.exp2(run * rates[n]) * starts[n] * splat_s[rows, n * 128 : (n + 1) * 128]
                for n in range(STATE)
            ]
            ready_s[j, rows, :] = tree_sum(terms) + y_ref[j, rows, :]
            return carry

        lax.fori_loop(0, TB, correct, 0, unroll=4)

    def gate_chunk(chunk, carry):
        for j in range(TILES):
            cols = slice(j * 128, (j + 1) * 128)
            ssm = ready_s.at[j][pl.ds(chunk, TB, stride=CHUNKS), :].astype(jnp.bfloat16).astype(jnp.float32)
            gate = gate_ref[chunk, :, cols].astype(jnp.float32)
            out_ref[chunk, :, cols] = (ssm * (gate * jax.nn.sigmoid(gate))).astype(jnp.bfloat16)
        return carry

    lax.fori_loop(0, CHUNKS, gate_chunk, 0)


def finish_call(info, y, cum, mix_out, spread, gate, rate, end, sums, every):
    f32 = jnp.float32
    whole = lambda shape: pl.BlockSpec(shape, lambda i, s: (0,) * len(shape))
    rows = TB * CHUNKS
    tiles = pl.BlockSpec((TILES, rows, 128), lambda i, s: (0, i, 0))
    return pl.pallas_call(
        finish_kernel,
        grid_spec=pltpu.PrefetchScalarGridSpec(
            num_scalar_prefetch=1,
            grid=(STEPS,),
            in_specs=[
                tiles, tiles, pl.BlockSpec((rows, STATE), lambda i, s: (i, 0)), whole((STATE, STATE * 128)),
                pl.BlockSpec((CHUNKS, TB, COLS), lambda i, s: (0, i, 0)),
                whole((STATE, COLS)), whole((TILES, CHUNKS * STATE, 128)), whole((TILES, CHUNKS, 128)),
                whole((2 * CHUNKS, TILES, 24, 128)),
            ],
            out_specs=pl.BlockSpec((CHUNKS, TB, COLS), lambda i, s: (0, i, 0)),
            scratch_shapes=[
                pltpu.VMEM((rows, STATE * 128), f32), pltpu.VMEM((TILES, CHUNKS * STATE, 128), f32),
                pltpu.VMEM((2 * CHUNKS, STATE, 128), f32), pltpu.VMEM((TILES, rows, 128), f32),
            ],
        ),
        out_shape=jax.ShapeDtypeStruct((CHUNKS, CLEN, COLS), jnp.bfloat16),
        compiler_params=pltpu.CompilerParams(vmem_limit_bytes=VMEM_LIMIT),
        cost_estimate=pl.CostEstimate(flops=50_000_000_000, bytes_accessed=16 * 2**20, transcendentals=0),
        name="finish_chunks",
    )(info, y, cum, mix_out, spread, gate, rate, end, sums, every)


QB = 256


def attention_kernel(side_ref, dev_ref, half_ref, diag_ref, first_ref, q_ref, kv_ref, o_ref, top_s, sum_s, acc_s):
    item = pl.program_id(0)
    scale = HD ** (-0.5) * LOG2E

    @pl.when(first_ref[item] == 1)
    def _():
        top_s[...] = jnp.full_like(top_s, NEG_LARGE)
        sum_s[...] = jnp.zeros_like(sum_s)
        acc_s[...] = jnp.zeros_like(acc_s)

    def absorb(masked):
        keys = kv_ref[0, :, 0, :, :HD].reshape(SPAN, HD)
        values = kv_ref[0, :, 0, :, HD:].reshape(SPAN, HD)
        for i in range(SPAN // QB):
            rows = slice(i * QB, (i + 1) * QB)
            scores = lax.dot_general(
                q_ref[0, rows, :], keys, (((1,), (1,)), ((), ())), preferred_element_type=jnp.float32
            ) * scale
            if masked:
                place = lax.broadcasted_iota(jnp.int32, (QB, SPAN), 1)
                key_pos = ((place // 64) % 4) * 256 + (place // 256) * 64 + place % 64
                query_pos = i * QB + lax.broadcasted_iota(jnp.int32, (QB, SPAN), 0)
                scores = jnp.where(key_pos <= query_pos, scores, NEG_LARGE)
            top = top_s[rows, :]
            new_top = jnp.maximum(top, jnp.max(scores, axis=1, keepdims=True))
            weights = jnp.exp2(scores - new_top[:, :1])
            shrink = jnp.exp2(top - new_top)
            top_s[rows, :] = new_top
            sum_s[rows, :] = sum_s[rows, :] * shrink + jnp.sum(weights, axis=1, keepdims=True)
            acc_s[rows, :] = acc_s[rows, :] * shrink + jnp.dot(
                weights.astype(jnp.bfloat16), values, preferred_element_type=jnp.float32
            )

    @pl.when(diag_ref[item] == 0)
    def _():
        absorb(False)

    @pl.when(diag_ref[item] == 1)
    def _():
        absorb(True)
        o_ref[0] = (acc_s[...] / sum_s[...]).astype(jnp.bfloat16)


def attention_call(side, dev, half, diag, first, q, kv):
    f32 = jnp.float32
    return pl.pallas_call(
        attention_kernel,
        grid_spec=pltpu.PrefetchScalarGridSpec(
            num_scalar_prefetch=5,
            grid=(17,),
            in_specs=[
                pl.BlockSpec((1, SPAN, HD), lambda i, side, dev, half, diag, first: (side[i], 0, 0)),
                pl.BlockSpec(
                    (1, 4, 1, 256, 2 * HD), lambda i, side, dev, half, diag, first: (dev[i], 0, half[i], 0, 0)
                ),
            ],
            out_specs=pl.BlockSpec((1, SPAN, HD), lambda i, side, dev, half, diag, first: (side[i], 0, 0)),
            scratch_shapes=[pltpu.VMEM((SPAN, 128), f32), pltpu.VMEM((SPAN, 128), f32), pltpu.VMEM((SPAN, HD), f32)],
        ),
        out_shape=jax.ShapeDtypeStruct((2, SPAN, HD), jnp.bfloat16),
        compiler_params=pltpu.CompilerParams(vmem_limit_bytes=VMEM_LIMIT),
        cost_estimate=pl.CostEstimate(flops=60_000_000_000, bytes_accessed=16 * 2**20, transcendentals=0),
        name="attend",
    )(side, dev, half, diag, first, q, kv)


ULYS = ("z", "w")
PLANE = ("blk", "w")


def small_gather(rows):
    return lax.all_gather(rows, "blk", axis=0, tiled=True)


def local(
    mamba_input, gate_input, delta_low, state_mixers, conv_weight, conv_bias, delta_weight, delta_bias,
    decay_log, skip_gain, queries, key_rows, value_rows, span_order,
):
    f32 = jnp.float32
    me = lax.axis_index("blk")
    places = jnp.arange(16, dtype=jnp.int32)
    holder = jnp.sum(jnp.where(span_order[None, :] == places[:, None], places[None, :], 0), axis=1)
    mine = lax.dynamic_slice_in_dim(span_order, 2 * me, 2, 0)

    x = lax.all_to_all(mamba_input, ULYS, split_axis=1, concat_axis=0, tiled=True)
    low_mix = lax.all_gather(
        jnp.concatenate([delta_low, state_mixers], axis=1), ULYS, axis=0, tiled=True
    )
    low = low_mix[:, :512].reshape(CHUNKS, CLEN, 512)
    mix = low_mix[:, 512:].reshape(CHUNKS, CLEN, 2 * STATE).swapaxes(0, 1).reshape(CHUNKS * CLEN, 2 * STATE)
    x = x.reshape(CHUNKS, CLEN, COLS)
    tails = small_gather(x[3::4, CLEN - 8 :, :])
    follows = (span_order[None, :] == mine[:, None] - 1).astype(jnp.bfloat16)
    before = jnp.einsum("cj,jtk->ctk", follows, tails, preferred_element_type=f32)
    ends = x[:, CLEN - 8 :, :].astype(f32)
    prior = jnp.concatenate([before[:1], ends[:3], before[1:], ends[4:7]], axis=0)
    spread = jnp.repeat(jnp.eye(2 * STATE, dtype=jnp.bfloat16), 128, axis=1)
    rate = -jnp.exp(decay_log) * LOG2E

    y, cum, end, sums, total = scan_call(
        x, prior, low, mix, spread, delta_weight, conv_weight.astype(f32), conv_bias[None, :],
        delta_bias[None, :], rate, skip_gain[None, :],
    )

    gate = lax.all_to_all(gate_input, ULYS, split_axis=1, concat_axis=0, tiled=True)
    query = lax.all_to_all(queries, ULYS, split_axis=1, concat_axis=0, tiled=True)
    kv = jnp.concatenate([key_rows.reshape(64, 8, HD), value_rows.reshape(64, 8, HD)], axis=2)
    kv = lax.all_to_all(kv.reshape(64, 8 * 2 * HD), "z", split_axis=1, concat_axis=0, tiled=True)
    kv = lax.all_gather(kv, PLANE, axis=0, tiled=True).reshape(8, 4, 2, 256, 2 * HD)

    items = jnp.arange(17, dtype=jnp.int32)
    second = (items > mine[0]).astype(jnp.int32)
    place = jnp.where(second == 1, items - mine[0] - 1, items)
    stored = jnp.sum(jnp.where(place[:, None] == span_order[None, :], places[None, :], 0), axis=1)
    diag = (place == jnp.where(second == 1, mine[1], mine[0])).astype(jnp.int32)
    first = (place == 0).astype(jnp.int32)
    attended = attention_call(
        second, stored // 2, stored % 2, diag, first, query.reshape(2, SPAN, HD), kv
    ).reshape(2 * SPAN, HD)

    every = small_gather(total)
    gated = finish_call(
        jnp.concatenate([holder, mine]), y, cum, mix[:, STATE:], spread[:STATE, : STATE * 128],
        gate.reshape(CHUNKS, CLEN, COLS), rate, end, sums, every,
    ).reshape(CHUNKS * CLEN, COLS)
    mamba_output = lax.all_to_all(gated, ULYS, split_axis=0, concat_axis=1, tiled=True)
    attention_output = lax.all_to_all(attended, ULYS, split_axis=0, concat_axis=1, tiled=True)
    return (mamba_output, attention_output)


def solution(mesh):
    tokens = P(("blk", "z", "w"), None)
    wide = P(None, ULYS)
    flat = P(ULYS)
    placed = (
        tokens, tokens, tokens, tokens, wide, flat, wide, flat, wide, flat, tokens, tokens, tokens, P(),
    )
    split_mesh = Mesh(mesh.devices.reshape(8, 8, 4), ("blk", "z", "w"))
    return jax.shard_map(
        local, mesh=split_mesh, in_specs=placed, out_specs=(tokens, tokens), check_vma=False
    )
```

```python
import functools

import jax
import jax.numpy as jnp
from jax import lax
from jax.experimental import pallas as pl
from jax.experimental.pallas import tpu as pltpu
from jax.sharding import Mesh, PartitionSpec as P

STATE = 16
CONV = 4
HD = 128
SPAN = 1024
CHUNKS = 8
CLEN = 256
COLS = 512
TILES = COLS // 128
TB = 32
STEPS = CLEN // TB
NEG_LARGE = -1e30
LOG2E = 1.4426950408889634
VMEM_LIMIT = 56 * 2**20


def tree_sum(terms):
    while len(terms) > 1:
        terms = [a + b for a, b in zip(terms[::2], terms[1::2])] + terms[len(terms) // 2 * 2 :]
    return terms[0]


def scan_kernel(
    x_ref, prior_ref, low_ref, mix_ref, spread_ref, w_ref, convw_ref, convb_ref, bias_ref, rate_ref, skip_ref,
    y_ref, cum_ref, end_ref, sum_ref,
    delta_s, dx_s, direct_s, splat_s, tail_s, state_s, run_s,
):
    step = pl.program_id(0)

    @pl.when(step == 0)
    def _():
        tail_s[...] = prior_ref[...]
        state_s[...] = jnp.zeros_like(state_s)
        run_s[...] = jnp.zeros_like(run_s)

    splat_s[...] = jnp.dot(mix_ref[...], spread_ref[...], preferred_element_type=jnp.float32)

    def prepare(chunk, carry):
        x = x_ref[chunk].astype(jnp.float32)
        padded = jnp.concatenate([tail_s[chunk], x], axis=0)
        mixed = convb_ref[...] + convw_ref[CONV - 1 : CONV, :] * x
        for k in range(CONV - 1):
            mixed = mixed + convw_ref[k : k + 1, :] * padded[8 - (CONV - 1) + k : 8 - (CONV - 1) + k + TB]
        tail_s[chunk] = x[TB - 8 :]
        driven = mixed * jax.nn.sigmoid(mixed)
        raw = jnp.dot(low_ref[chunk], w_ref[...], preferred_element_type=jnp.float32) + bias_ref[...]
        delta = jnp.maximum(raw, 0.0) + jnp.log1p(jnp.exp(-jnp.abs(raw)))
        dx = delta * driven
        direct = skip_ref[...] * driven
        for j in range(TILES):
            cols = slice(j * 128, (j + 1) * 128)
            rows = pl.ds(chunk, TB, stride=CHUNKS)
            delta_s.at[j][rows, :] = delta[:, cols]
            dx_s.at[j][rows, :] = dx[:, cols]
            direct_s.at[j][rows, :] = direct[:, cols]
        return carry

    lax.fori_loop(0, CHUNKS, prepare, 0)

    for j in range(TILES):
        cols = slice(j * 128, (j + 1) * 128)
        rates = [jnp.broadcast_to(rate_ref[n : n + 1, cols], (CHUNKS, 128)) for n in range(STATE)]

        def advance(t, carry):
            hidden, run = carry
            rows = pl.ds(pl.multiple_of(t * CHUNKS, CHUNKS), CHUNKS)
            delta = delta_s[j, rows, :]
            dx = dx_s[j, rows, :]
            hidden = tuple(
                jnp.exp2(delta * rates[n]) * hidden[n] + dx * splat_s[rows, n * 128 : (n + 1) * 128]
                for n in range(STATE)
            )
            terms = [
                hidden[n] * splat_s[rows, (STATE + n) * 128 : (STATE + n + 1) * 128] for n in range(STATE)
            ]
            run = run + delta
            y_ref[j, rows, :] = tree_sum(terms) + direct_s[j, rows, :]
            cum_ref[j, rows, :] = run
            return (hidden, run)

        hidden, run = lax.fori_loop(
            0, TB, advance, (tuple(state_s[j, n] for n in range(STATE)), run_s[j]), unroll=4
        )
        for n in range(STATE):
            state_s[j, n] = hidden[n]
        run_s[j] = run

    @pl.when(step == STEPS - 1)
    def _():
        for j in range(TILES):
            for n in range(STATE):
                end_ref.at[j][pl.ds(n, CHUNKS, stride=STATE), :] = state_s[j, n]
            sum_ref[j] = run_s[j]


def scan_call(x, prior, low, mix, spread, w, convw, convb, bias, rate, skip):
    f32 = jnp.float32
    whole = lambda shape: pl.BlockSpec(shape, lambda i: (0,) * len(shape))
    tokens = lambda width: pl.BlockSpec((CHUNKS, TB, width), lambda i: (0, i, 0))
    rows = TB * CHUNKS
    return pl.pallas_call(
        scan_kernel,
        grid=(STEPS,),
        in_specs=[
            tokens(COLS), whole((CHUNKS, 8, COLS)), tokens(512),
            pl.BlockSpec((rows, 2 * STATE), lambda i: (i, 0)), whole((2 * STATE, 2 * STATE * 128)),
            whole((512, COLS)), whole((CONV, COLS)), whole((1, COLS)), whole((1, COLS)),
            whole((STATE, COLS)), whole((1, COLS)),
        ],
        out_specs=[
            pl.BlockSpec((TILES, rows, 128), lambda i: (0, i, 0)),
            pl.BlockSpec((TILES, rows, 128), lambda i: (0, i, 0)),
            whole((TILES, CHUNKS * STATE, 128)), whole((TILES, CHUNKS, 128)),
        ],
        out_shape=[
            jax.ShapeDtypeStruct((TILES, CLEN * CHUNKS, 128), f32),
            jax.ShapeDtypeStruct((TILES, CLEN * CHUNKS, 128), f32),
            jax.ShapeDtypeStruct((TILES, CHUNKS * STATE, 128), f32),
            jax.ShapeDtypeStruct((TILES, CHUNKS, 128), f32),
        ],
        scratch_shapes=[
            pltpu.VMEM((TILES, rows, 128), f32), pltpu.VMEM((TILES, rows, 128), f32),
            pltpu.VMEM((TILES, rows, 128), f32), pltpu.VMEM((rows, 2 * STATE * 128), f32),
            pltpu.VMEM((CHUNKS, 8, COLS), f32), pltpu.VMEM((TILES, STATE, CHUNKS, 128), f32),
            pltpu.VMEM((TILES, CHUNKS, 128), f32),
        ],
        compiler_params=pltpu.CompilerParams(vmem_limit_bytes=VMEM_LIMIT),
        cost_estimate=pl.CostEstimate(flops=100_000_000_000, bytes_accessed=16 * 2**20, transcendentals=0),
        name="scan_chunks",
    )(x, prior, low, mix, spread, w, convw, convb, bias, rate, skip)


def finish_kernel(y_ref, cum_ref, mix_ref, spread_ref, gate_ref, rate_ref, start_ref, out_ref, splat_s, ready_s):
    splat_s[...] = jnp.dot(mix_ref[...], spread_ref[...], preferred_element_type=jnp.float32)

    for j in range(TILES):
        cols = slice(j * 128, (j + 1) * 128)
        rates = [jnp.broadcast_to(rate_ref[n : n + 1, cols], (CHUNKS, 128)) for n in range(STATE)]
        starts = [start_ref.at[j][pl.ds(n, CHUNKS, stride=STATE), :] for n in range(STATE)]

        def correct(t, carry):
            rows = pl.ds(pl.multiple_of(t * CHUNKS, CHUNKS), CHUNKS)
            run = cum_ref[j, rows, :]
            terms = [
                jnp.exp2(run * rates[n]) * starts[n] * splat_s[rows, n * 128 : (n + 1) * 128]
                for n in range(STATE)
            ]
            ready_s[j, rows, :] = tree_sum(terms) + y_ref[j, rows, :]
            return carry

        lax.fori_loop(0, TB, correct, 0, unroll=4)

    def gate_chunk(chunk, carry):
        for j in range(TILES):
            cols = slice(j * 128, (j + 1) * 128)
            ssm = ready_s.at[j][pl.ds(chunk, TB, stride=CHUNKS), :].astype(jnp.bfloat16).astype(jnp.float32)
            gate = gate_ref[chunk, :, cols].astype(jnp.float32)
            out_ref[chunk, :, cols] = (ssm * (gate * jax.nn.sigmoid(gate))).astype(jnp.bfloat16)
        return carry

    lax.fori_loop(0, CHUNKS, gate_chunk, 0)


def finish_call(y, cum, mix_out, spread, gate, rate, starts):
    f32 = jnp.float32
    whole = lambda shape: pl.BlockSpec(shape, lambda i: (0,) * len(shape))
    rows = TB * CHUNKS
    tiles = pl.BlockSpec((TILES, rows, 128), lambda i: (0, i, 0))
    tokens = pl.BlockSpec((CHUNKS, TB, COLS), lambda i: (0, i, 0))
    return pl.pallas_call(
        finish_kernel,
        grid=(STEPS,),
        in_specs=[
            tiles, tiles, pl.BlockSpec((rows, STATE), lambda i: (i, 0)), whole((STATE, STATE * 128)), tokens,
            whole((STATE, COLS)), whole((TILES, CHUNKS * STATE, 128)),
        ],
        out_specs=tokens,
        out_shape=jax.ShapeDtypeStruct((CHUNKS, CLEN, COLS), jnp.bfloat16),
        scratch_shapes=[pltpu.VMEM((rows, STATE * 128), f32), pltpu.VMEM((TILES, rows, 128), f32)],
        compiler_params=pltpu.CompilerParams(vmem_limit_bytes=VMEM_LIMIT),
        cost_estimate=pl.CostEstimate(flops=50_000_000_000, bytes_accessed=16 * 2**20, transcendentals=0),
        name="finish_chunks",
    )(y, cum, mix_out, spread, gate, rate, starts)


QB = 256


def attention_kernel(side_ref, dev_ref, half_ref, diag_ref, first_ref, q_ref, kv_ref, o_ref, top_s, sum_s, acc_s):
    item = pl.program_id(0)
    scale = HD ** (-0.5) * LOG2E

    @pl.when(first_ref[item] == 1)
    def _():
        top_s[...] = jnp.full_like(top_s, NEG_LARGE)
        sum_s[...] = jnp.zeros_like(sum_s)
        acc_s[...] = jnp.zeros_like(acc_s)

    def absorb(masked):
        keys = kv_ref[0, :, 0, :, :HD].reshape(SPAN, HD)
        values = kv_ref[0, :, 0, :, HD:].reshape(SPAN, HD)
        for i in range(SPAN // QB):
            rows = slice(i * QB, (i + 1) * QB)
            scores = lax.dot_general(
                q_ref[0, rows, :], keys, (((1,), (1,)), ((), ())), preferred_element_type=jnp.float32
            ) * scale
            if masked:
                place = lax.broadcasted_iota(jnp.int32, (QB, SPAN), 1)
                key_pos = ((place // 64) % 4) * 256 + (place // 256) * 64 + place % 64
                query_pos = i * QB + lax.broadcasted_iota(jnp.int32, (QB, SPAN), 0)
                scores = jnp.where(key_pos <= query_pos, scores, NEG_LARGE)
            top = top_s[rows, :]
            new_top = jnp.maximum(top, jnp.max(scores, axis=1, keepdims=True))
            weights = jnp.exp2(scores - new_top[:, :1])
            shrink = jnp.exp2(top - new_top)
            top_s[rows, :] = new_top
            sum_s[rows, :] = sum_s[rows, :] * shrink + jnp.sum(weights, axis=1, keepdims=True)
            acc_s[rows, :] = acc_s[rows, :] * shrink + jnp.dot(
                weights.astype(jnp.bfloat16), values, preferred_element_type=jnp.float32
            )

    @pl.when(diag_ref[item] == 0)
    def _():
        absorb(False)

    @pl.when(diag_ref[item] == 1)
    def _():
        absorb(True)
        o_ref[0] = (acc_s[...] / sum_s[...]).astype(jnp.bfloat16)


def attention_call(side, dev, half, diag, first, q, kv):
    f32 = jnp.float32
    return pl.pallas_call(
        attention_kernel,
        grid_spec=pltpu.PrefetchScalarGridSpec(
            num_scalar_prefetch=5,
            grid=(17,),
            in_specs=[
                pl.BlockSpec((1, SPAN, HD), lambda i, side, dev, half, diag, first: (side[i], 0, 0)),
                pl.BlockSpec(
                    (1, 4, 1, 256, 2 * HD), lambda i, side, dev, half, diag, first: (dev[i], 0, half[i], 0, 0)
                ),
            ],
            out_specs=pl.BlockSpec((1, SPAN, HD), lambda i, side, dev, half, diag, first: (side[i], 0, 0)),
            scratch_shapes=[pltpu.VMEM((SPAN, 128), f32), pltpu.VMEM((SPAN, 128), f32), pltpu.VMEM((SPAN, HD), f32)],
        ),
        out_shape=jax.ShapeDtypeStruct((2, SPAN, HD), jnp.bfloat16),
        compiler_params=pltpu.CompilerParams(vmem_limit_bytes=VMEM_LIMIT),
        cost_estimate=pl.CostEstimate(flops=60_000_000_000, bytes_accessed=16 * 2**20, transcendentals=0),
        name="attend",
    )(side, dev, half, diag, first, q, kv)


WIDE = 640
TAIL = 16
MESH = pl.DeviceIdType.MESH


def intake_kernel(
    x_ref, low_ref, kv_ref, weight_ref, params_ref, x_out, low_out, tail_out, kv_out, weight_out, params_out, weight_mid, params_mid,
    own_sem, kv_send, kv_recv, swap_send, swap_recv, x_send, x_recv, low_send, low_recv, col_send, col_recv, tail_send, tail_recv,
):
    blk, z, w = lax.axis_index("blk"), lax.axis_index("z"), lax.axis_index("w")
    me = blk * 4 + w
    barrier = pltpu.get_barrier_semaphore()

    def greet(k, carry):
        peer = lax.rem(me + k, 32)
        pl.semaphore_signal(barrier, inc=1, device_id=(peer // 4, z, lax.rem(peer, 4)), device_id_type=MESH)
        return carry

    def greet_z(k, carry):
        pl.semaphore_signal(barrier, inc=1, device_id=(blk, lax.rem(z + k, 8), w), device_id_type=MESH)
        return carry

    lax.fori_loop(1, 32, greet, 0)
    lax.fori_loop(1, 8, greet_z, 0)

    pl.semaphore_wait(barrier, 38)

    def kv_copy(k):
        peer = lax.rem(z + k, 8)
        return pltpu.make_async_remote_copy(
            src_ref=kv_ref.at[:, pl.ds(pl.multiple_of(peer * 2 * HD, 2 * HD), 2 * HD)], dst_ref=kv_out.at[z],
            send_sem=kv_send.at[k], recv_sem=kv_recv.at[z], device_id=(blk, peer, w), device_id_type=MESH,
        )

    shift = lax.rem(blk - z + 8, 8)
    held, middle, settled = (weight_ref, params_ref), (weight_mid, params_mid), (weight_out, params_out)

    def along(slot):
        return pltpu.make_async_remote_copy(
            src_ref=held[slot], dst_ref=middle[slot], send_sem=swap_send.at[slot], recv_sem=swap_recv.at[slot],
            device_id=(blk, shift, w), device_id_type=MESH,
        )

    def along_here(slot):
        return pltpu.make_async_copy(held[slot], middle[slot], swap_recv.at[slot])

    def across_plane(slot):
        return pltpu.make_async_remote_copy(
            src_ref=middle[slot], dst_ref=settled[slot], send_sem=swap_send.at[2 + slot],
            recv_sem=swap_recv.at[2 + slot], device_id=(shift, z, w), device_id_type=MESH,
        )

    def across_here(slot):
        return pltpu.make_async_copy(middle[slot], settled[slot], swap_recv.at[2 + slot])

    def low_copy(k):
        return pltpu.make_async_remote_copy(
            src_ref=low_ref, dst_ref=low_out.at[blk, w], send_sem=low_send.at[k], recv_sem=low_recv.at[blk],
            device_id=(lax.rem(blk + k, 8), z, w), device_id_type=MESH,
        )

    def x_copy(k):
        peer = lax.rem(me + 1 + lax.rem(k - 1 + 11 * me, 31), 32)
        return pltpu.make_async_remote_copy(
            src_ref=x_ref.at[:, pl.ds(pl.multiple_of(peer * COLS, COLS), COLS)], dst_ref=x_out.at[blk, w],
            send_sem=x_send.at[k], recv_sem=x_recv.at[me],
            device_id=(peer // 4, z, lax.rem(peer, 4)), device_id_type=MESH,
        )

    def x_arrival(source):
        return pltpu.make_async_remote_copy(
            src_ref=x_out.at[source // 4, lax.rem(source, 4)], dst_ref=x_out.at[source // 4, lax.rem(source, 4)],
            send_sem=x_send.at[0],
            recv_sem=x_recv.at[source], device_id=(blk, z, w), device_id_type=MESH,
        )

    def start(copy):
        def go(k, carry):
            copy(k).start()
            return carry

        return go

    own_low = pltpu.make_async_copy(low_ref, low_out.at[blk, w], own_sem.at[0])
    own_x = pltpu.make_async_copy(
        x_ref.at[:, pl.ds(pl.multiple_of(me * COLS, COLS), COLS)], x_out.at[blk, w], own_sem.at[1]
    )
    own_low.start()
    lax.fori_loop(1, 8, start(low_copy), 0)
    own_kv = pltpu.make_async_copy(
        kv_ref.at[:, pl.ds(pl.multiple_of(z * 2 * HD, 2 * HD), 2 * HD)], kv_out.at[z], own_sem.at[2]
    )

    @pl.when(shift != z)
    def _():
        along(0).start()
        along(1).start()

    @pl.when(shift == z)
    def _():
        along_here(0).start()
        along_here(1).start()

    own_x.start()
    own_kv.start()
    lax.fori_loop(1, 12, start(x_copy), 0)
    lax.fori_loop(1, 8, start(kv_copy), 0)

    def low_arrived(k, carry):
        source = lax.rem(blk + k, 8)
        pltpu.make_async_remote_copy(
            src_ref=low_out.at[source, w], dst_ref=low_out.at[source, w], send_sem=low_send.at[0],
            recv_sem=low_recv.at[source], device_id=(blk, z, w), device_id_type=MESH,
        ).wait_recv()
        return carry

    own_low.wait()
    lax.fori_loop(1, 8, low_arrived, 0)
    across = lax.rem(w + 2, 4)
    sibling = (w // 2) * 2 + 1 - lax.rem(w, 2)
    sibling_across = lax.rem(sibling + 2, 4)

    def column(which, slot, target):
        return pltpu.make_async_remote_copy(
            src_ref=low_out.at[:, which], dst_ref=low_out.at[:, which], send_sem=col_send.at[slot],
            recv_sem=col_recv.at[slot], device_id=(blk, z, target), device_id_type=MESH,
        )

    over = column(w, 0, across)
    beside = column(w, 1, sibling)
    over.start()
    beside.start()
    lax.fori_loop(12, 32, start(x_copy), 0)

    @pl.when(shift != z)
    def _():
        for slot in range(2):
            along(slot).wait_recv()
            along(slot).wait_send()

    @pl.when(shift == z)
    def _():
        along_here(0).wait()
        along_here(1).wait()

    @pl.when(z != 0)
    def _():
        across_plane(0).start()
        across_plane(1).start()

    @pl.when(z == 0)
    def _():
        across_here(0).start()
        across_here(1).start()
    column(across, 0, across).wait_recv()
    relay = column(across, 2, sibling)
    relay.start()

    own_x.wait()

    def wait_x(k, carry):
        x_arrival(lax.rem(me + k, 32)).wait_recv()
        return carry

    lax.fori_loop(1, 32, wait_x, 0)

    part, quarter = z // 4, lax.rem(z, 4)

    def tail_copy(slot, which, target):
        return pltpu.make_async_remote_copy(
            src_ref=x_out.at[:, 3, pl.ds(64 - TAIL, TAIL)], dst_ref=tail_out.at[slot],
            send_sem=tail_send.at[which], recv_sem=tail_recv.at[slot],
            device_id=(blk, target, w), device_id_type=MESH,
        )

    @pl.when(quarter != 3)
    def _():
        tail_copy(0, 0, lax.rem(z + 1, 8)).start()

    @pl.when(quarter == 3)
    def _():
        tail_copy(part, 0, 0).start()
        tail_copy(part, 1, 4).start()

    column(sibling, 1, sibling).wait_recv()
    column(sibling_across, 2, sibling).wait_recv()

    @pl.when(quarter != 0)
    def _():
        tail_copy(0, 0, lax.rem(z + 1, 8)).wait_recv()

    @pl.when(quarter == 0)
    def _():
        tail_copy(0, 0, lax.rem(z + 1, 8)).wait_recv()
        tail_copy(1, 0, lax.rem(z + 1, 8)).wait_recv()

    tail_copy(0, 0, lax.rem(z + 1, 8)).wait_send()

    @pl.when(quarter == 3)
    def _():
        tail_copy(0, 1, lax.rem(z + 1, 8)).wait_send()

    def low_sent(k, carry):
        low_copy(k).wait_send()
        return carry

    def x_sent(k, carry):
        x_copy(k).wait_send()
        return carry

    own_kv.wait()

    def kv_done(k, carry):
        source = lax.rem(z + k, 8)
        pltpu.make_async_remote_copy(
            src_ref=kv_out.at[source], dst_ref=kv_out.at[source], send_sem=kv_send.at[0],
            recv_sem=kv_recv.at[source], device_id=(blk, z, w), device_id_type=MESH,
        ).wait_recv()
        kv_copy(k).wait_send()
        return carry

    lax.fori_loop(1, 8, kv_done, 0)

    @pl.when(z != 0)
    def _():
        for slot in range(2):
            across_plane(slot).wait_recv()
            across_plane(slot).wait_send()

    @pl.when(z == 0)
    def _():
        across_here(0).wait()
        across_here(1).wait()

    lax.fori_loop(1, 8, low_sent, 0)
    lax.fori_loop(1, 32, x_sent, 0)
    over.wait_send()
    beside.wait_send()
    relay.wait_send()


def intake_call(x, low, kv, weight, params):
    anywhere = pl.BlockSpec(memory_space=pl.ANY)
    sems = pltpu.SemaphoreType.DMA
    return pl.pallas_call(
        intake_kernel,
        in_specs=[anywhere] * 5,
        out_specs=[anywhere] * 8,
        out_shape=[
            jax.ShapeDtypeStruct((8, 4, 64, COLS), jnp.bfloat16),
            jax.ShapeDtypeStruct((8, 4, 64, WIDE), jnp.bfloat16),
            jax.ShapeDtypeStruct((2, 8, TAIL, COLS), jnp.bfloat16),
            jax.ShapeDtypeStruct((8, 64, 2 * HD), jnp.bfloat16),
            jax.ShapeDtypeStruct(weight.shape, weight.dtype),
            jax.ShapeDtypeStruct(params.shape, params.dtype),
            jax.ShapeDtypeStruct(weight.shape, weight.dtype),
            jax.ShapeDtypeStruct(params.shape, params.dtype),
        ],
        scratch_shapes=[
            sems((3,)), sems((8,)), sems((8,)), sems((4,)), sems((4,)), sems((32,)), sems((32,)), sems((8,)), sems((8,)),
            sems((3,)), sems((3,)),
            sems((2,)), sems((2,)),
        ],
        compiler_params=pltpu.CompilerParams(collective_id=0, has_side_effects=True),
        name="intake",
    )(x, low, kv, weight, params)


def states_kernel(
    order_ref, end_ref, sum_ref, rate_ref, start_ref,
    got_end, got_sum, chain, reply, own_sem, end_send, end_recv, sum_send, sum_recv, back_send, back_recv,
):
    blk, z, w = lax.axis_index("blk"), lax.axis_index("z"), lax.axis_index("w")
    barrier = pltpu.get_barrier_semaphore()

    def greet(k, carry):
        pl.semaphore_signal(barrier, inc=1, device_id=(blk, lax.rem(z + k, 8), w), device_id_type=MESH)
        return carry

    lax.fori_loop(1, 8, greet, 0)
    pl.semaphore_wait(barrier, 7)
    mine = pl.ds(pl.multiple_of(z * 8, 8), 8)

    def remote(src, dst, send, recv, target):
        return pltpu.make_async_remote_copy(
            src_ref=src, dst_ref=dst, send_sem=send, recv_sem=recv, device_id=(blk, target, w), device_id_type=MESH
        )

    def end_copy(k):
        peer = lax.rem(z + k, 8)
        return remote(
            end_ref.at[peer // 2, :, lax.rem(peer, 2)], got_end.at[mine], end_send.at[k], end_recv.at[z], peer
        )

    def sum_copy(k):
        peer = lax.rem(z + k, 8)
        return remote(sum_ref.at[peer // 2], got_sum.at[mine], sum_send.at[k], sum_recv.at[z], peer)

    def back_copy(k):
        peer = lax.rem(z + k, 8)
        return remote(
            reply.at[pl.ds(pl.multiple_of(peer * 8, 8), 8)], start_ref.at[z // 2, :, lax.rem(z, 2)],
            back_send.at[k], back_recv.at[z], peer,
        )

    def send_ends(k, carry):
        end_copy(k).start()
        sum_copy(k).start()
        return carry

    lax.fori_loop(1, 8, send_ends, 0)
    own_end = pltpu.make_async_copy(end_ref.at[z // 2, :, lax.rem(z, 2)], got_end.at[mine], own_sem.at[0])
    own_sum = pltpu.make_async_copy(sum_ref.at[z // 2], got_sum.at[mine], own_sem.at[1])
    own_end.start()
    own_sum.start()
    own_end.wait()
    own_sum.wait()

    def ends_arrived(k, carry):
        source = lax.rem(z + k, 8)
        there = pl.ds(pl.multiple_of(source * 8, 8), 8)
        remote(got_end.at[there], got_end.at[there], end_send.at[0], end_recv.at[source], z).wait_recv()
        remote(got_sum.at[there], got_sum.at[there], sum_send.at[0], sum_recv.at[source], z).wait_recv()
        return carry

    lax.fori_loop(1, 8, ends_arrived, 0)
    rate = rate_ref[z // 2, lax.rem(z, 2)]

    def carry_on(position, state):
        chain[position] = state
        index = order_ref[position]
        return jnp.exp2(rate * got_sum[pl.ds(index, 1), :]) * state + got_end[index]

    lax.fori_loop(0, 64, carry_on, jnp.zeros((8, 128), jnp.float32))

    def pick(index, carry):
        reply[index] = chain[order_ref[64 + index]]
        return carry

    lax.fori_loop(0, 64, pick, 0)

    def send_back(k, carry):
        back_copy(k).start()
        return carry

    lax.fori_loop(1, 8, send_back, 0)
    own_back = pltpu.make_async_copy(reply.at[mine], start_ref.at[z // 2, :, lax.rem(z, 2)], own_sem.at[2])
    own_back.start()
    own_back.wait()

    def finish(k, carry):
        source = lax.rem(z + k, 8)
        landed = start_ref.at[source // 2, :, lax.rem(source, 2)]
        remote(landed, landed, back_send.at[0], back_recv.at[source], z).wait_recv()
        end_copy(k).wait_send()
        sum_copy(k).wait_send()
        back_copy(k).wait_send()
        return carry

    lax.fori_loop(1, 8, finish, 0)


def states_call(order, ends, sums, rate):
    f32 = jnp.float32
    here = pl.BlockSpec(memory_space=pltpu.VMEM)
    sems = pltpu.SemaphoreType.DMA
    return pl.pallas_call(
        states_kernel,
        in_specs=[pl.BlockSpec(memory_space=pltpu.SMEM), here, here, here],
        out_specs=here,
        out_shape=jax.ShapeDtypeStruct((TILES, CHUNKS, 2, 8, 128), f32),
        scratch_shapes=[
            pltpu.VMEM((64, 8, 128), f32), pltpu.VMEM((64, 128), f32), pltpu.VMEM((64, 8, 128), f32),
            pltpu.VMEM((64, 8, 128), f32), sems((3,)), sems((8,)), sems((8,)), sems((8,)), sems((8,)),
            sems((8,)), sems((8,)),
        ],
        compiler_params=pltpu.CompilerParams(collective_id=1, has_side_effects=True),
        name="chain_states",
    )(order, ends, sums, rate)


ULYS = ("z", "w")
PLANE = ("blk", "w")


def local(
    mamba_input, gate_input, delta_low, state_mixers, conv_weight, conv_bias, delta_weight, delta_bias,
    decay_log, skip_gain, queries, key_rows, value_rows, span_order,
):
    f32 = jnp.float32
    me, z = lax.axis_index("blk"), lax.axis_index("z")
    zpart = z // 4
    params = jnp.concatenate(
        [
            -jnp.exp(decay_log) * LOG2E, conv_weight.astype(f32), conv_bias[None, :], delta_bias[None, :],
            skip_gain[None, :], jnp.zeros((1, COLS), f32),
        ],
        axis=0,
    )
    places = jnp.arange(16, dtype=jnp.int32)
    mine = lax.dynamic_slice_in_dim(span_order, 2 * me, 2, 0)

    low_mix = jnp.concatenate(
        [delta_low, state_mixers, jnp.zeros((64, WIDE - 512 - 2 * STATE), jnp.bfloat16)], axis=1
    )
    kv = jnp.concatenate([key_rows.reshape(64, 8, HD), value_rows.reshape(64, 8, HD)], axis=2)
    x, low_mix, tails, kv, weight, params, _, _ = intake_call(
        mamba_input, low_mix, kv.reshape(64, 8 * 2 * HD), delta_weight, params
    )
    x, gate_input, queries = lax.optimization_barrier((x, gate_input, queries))
    rate = params[:STATE]
    low = low_mix.reshape(CHUNKS, CLEN, WIDE)
    mix = (
        low[:, :, 512 : 512 + 2 * STATE].swapaxes(0, 1).reshape(CHUNKS * CLEN, 2 * STATE)
    )
    x = x.reshape(CHUNKS, CLEN, COLS)
    places = places[:, None]
    earlier = span_order.reshape(CHUNKS, 2)[:, zpart] - 1
    follows = (earlier[:, None] == span_order[None, :]).astype(jnp.bfloat16)
    at_start = lax.rem(z, 4) == 0
    tails = tails[:, :, TAIL - 8 :]
    of_block = tails.swapaxes(0, 1).reshape(16, 8, COLS)
    before = jnp.einsum("cj,jtk->ctk", follows, of_block, preferred_element_type=f32)
    prior = jnp.where(at_start, before, tails[0].astype(f32))
    spread = jnp.repeat(jnp.eye(2 * STATE, dtype=jnp.bfloat16), 128, axis=1)

    y, cum, end, sums = scan_call(
        x, prior, low, mix, spread, weight, params[16:20], params[20:21], params[21:22], rate, params[22:23],
    )

    gate = lax.all_to_all(gate_input, PLANE, split_axis=1, concat_axis=0, tiled=True)
    query = lax.all_to_all(queries, ULYS, split_axis=1, concat_axis=0, tiled=True)
    kv = lax.all_gather(kv.reshape(512, 2 * HD), PLANE, axis=0, tiled=True).reshape(8, 4, 2, 256, 2 * HD)

    items = jnp.arange(17, dtype=jnp.int32)
    second = (items > mine[0]).astype(jnp.int32)
    place = jnp.where(second == 1, items - mine[0] - 1, items)
    stored = jnp.sum(jnp.where(place[:, None] == span_order[None, :], places.T, 0), axis=1)
    diag = (place == jnp.where(second == 1, mine[1], mine[0])).astype(jnp.int32)
    first = (place == 0).astype(jnp.int32)
    attended = attention_call(
        second, stored // 2, stored % 2, diag, first, query.reshape(2, SPAN, HD), kv
    ).reshape(2 * SPAN, HD)

    steps = jnp.arange(64, dtype=jnp.int32)
    at = jnp.sum(jnp.where((steps // 4)[:, None] == span_order[None, :], places.T, 0), axis=1)
    index_of = ((at % 2) * 4 + steps % 4) * 8 + at // 2
    block_of = 2 * (steps % 8) + steps // 32
    place_of = jnp.sum(jnp.where(block_of[:, None] == places.T, span_order[None, :], 0), axis=1)
    position_of = place_of * 4 + (steps // 8) % 4
    starts = states_call(
        jnp.concatenate([index_of, position_of]), end.reshape(TILES, CHUNKS, 2, 8, 128), sums,
        rate.reshape(2, 8, TILES, 128).transpose(2, 0, 1, 3),
    )
    gated = finish_call(
        y, cum, mix[:, STATE:], spread[:STATE, : STATE * 128], gate.reshape(CHUNKS, CLEN, COLS), rate,
        starts.reshape(TILES, CHUNKS * STATE, 128),
    ).reshape(CHUNKS * CLEN, COLS)
    mamba_output = lax.all_to_all(gated, PLANE, split_axis=0, concat_axis=1, tiled=True)
    attention_output = lax.all_to_all(attended, ULYS, split_axis=0, concat_axis=1, tiled=True)
    return (mamba_output, attention_output)


def solution(mesh):
    tokens = P(("blk", "z", "w"), None)
    wide = P(None, ULYS)
    flat = P(ULYS)
    placed = (
        tokens, tokens, tokens, tokens, wide, flat, wide, flat, wide, flat, tokens, tokens, tokens, P(),
    )
    split_mesh = Mesh(mesh.devices.reshape(8, 8, 4), ("blk", "z", "w"))
    return jax.shard_map(
        local, mesh=split_mesh, in_specs=placed, out_specs=(tokens, tokens), check_vma=False
    )
```

```python
import functools

import jax
import jax.numpy as jnp
from jax import lax
from jax.experimental import pallas as pl
from jax.experimental.pallas import tpu as pltpu
from jax.sharding import Mesh, PartitionSpec as P

STATE = 16
CONV = 4
HD = 128
SPAN = 1024
CHUNKS = 8
CLEN = 256
COLS = 512
TILES = COLS // 128
TB = 32
STEPS = CLEN // TB
NEG_LARGE = -1e30
LOG2E = 1.4426950408889634
VMEM_LIMIT = 56 * 2**20


def tree_sum(terms):
    while len(terms) > 1:
        terms = [a + b for a, b in zip(terms[::2], terms[1::2])] + terms[len(terms) // 2 * 2 :]
    return terms[0]


def scan_kernel(
    x_ref, prior_ref, low_ref, mix_ref, spread_ref, w_ref, convw_ref, convb_ref, bias_ref, rate_ref, skip_ref,
    y_ref, cum_ref, end_ref, sum_ref,
    delta_s, dx_s, direct_s, splat_s, tail_s, state_s, run_s,
):
    step = pl.program_id(0)

    @pl.when(step == 0)
    def _():
        tail_s[...] = prior_ref[...]
        state_s[...] = jnp.zeros_like(state_s)
        run_s[...] = jnp.zeros_like(run_s)

    splat_s[...] = jnp.dot(mix_ref[...], spread_ref[...], preferred_element_type=jnp.float32)

    def prepare(chunk, carry):
        x = x_ref[chunk].astype(jnp.float32)
        padded = jnp.concatenate([tail_s[chunk], x], axis=0)
        mixed = convb_ref[...] + convw_ref[CONV - 1 : CONV, :] * x
        for k in range(CONV - 1):
            mixed = mixed + convw_ref[k : k + 1, :] * padded[8 - (CONV - 1) + k : 8 - (CONV - 1) + k + TB]
        tail_s[chunk] = x[TB - 8 :]
        driven = mixed * jax.nn.sigmoid(mixed)
        raw = jnp.dot(low_ref[chunk], w_ref[...], preferred_element_type=jnp.float32) + bias_ref[...]
        delta = jnp.maximum(raw, 0.0) + jnp.log1p(jnp.exp(-jnp.abs(raw)))
        dx = delta * driven
        direct = skip_ref[...] * driven
        for j in range(TILES):
            cols = slice(j * 128, (j + 1) * 128)
            rows = pl.ds(chunk, TB, stride=CHUNKS)
            delta_s.at[j][rows, :] = delta[:, cols]
            dx_s.at[j][rows, :] = dx[:, cols]
            direct_s.at[j][rows, :] = direct[:, cols]
        return carry

    lax.fori_loop(0, CHUNKS, prepare, 0)

    for j in range(TILES):
        cols = slice(j * 128, (j + 1) * 128)
        rates = [jnp.broadcast_to(rate_ref[n : n + 1, cols], (CHUNKS, 128)) for n in range(STATE)]

        def advance(t, carry):
            hidden, run = carry
            rows = pl.ds(pl.multiple_of(t * CHUNKS, CHUNKS), CHUNKS)
            delta = delta_s[j, rows, :]
            dx = dx_s[j, rows, :]
            hidden = tuple(
                jnp.exp2(delta * rates[n]) * hidden[n] + dx * splat_s[rows, n * 128 : (n + 1) * 128]
                for n in range(STATE)
            )
            terms = [
                hidden[n] * splat_s[rows, (STATE + n) * 128 : (STATE + n + 1) * 128] for n in range(STATE)
            ]
            run = run + delta
            y_ref[j, rows, :] = tree_sum(terms) + direct_s[j, rows, :]
            cum_ref[j, rows, :] = run
            return (hidden, run)

        hidden, run = lax.fori_loop(
            0, TB, advance, (tuple(state_s[j, n] for n in range(STATE)), run_s[j]), unroll=8
        )
        for n in range(STATE):
            state_s[j, n] = hidden[n]
        run_s[j] = run

    @pl.when(step == STEPS - 1)
    def _():
        for j in range(TILES):
            for n in range(STATE):
                end_ref.at[j][pl.ds(n, CHUNKS, stride=STATE), :] = state_s[j, n]
            sum_ref[j] = run_s[j]


def scan_call(x, prior, low, mix, spread, w, convw, convb, bias, rate, skip):
    f32 = jnp.float32
    whole = lambda shape: pl.BlockSpec(shape, lambda i: (0,) * len(shape))
    tokens = lambda width: pl.BlockSpec((CHUNKS, TB, width), lambda i: (0, i, 0))
    rows = TB * CHUNKS
    return pl.pallas_call(
        scan_kernel,
        grid=(STEPS,),
        in_specs=[
            tokens(COLS), whole((CHUNKS, 8, COLS)), tokens(512),
            pl.BlockSpec((rows, 2 * STATE), lambda i: (i, 0)), whole((2 * STATE, 2 * STATE * 128)),
            whole((512, COLS)), whole((CONV, COLS)), whole((1, COLS)), whole((1, COLS)),
            whole((STATE, COLS)), whole((1, COLS)),
        ],
        out_specs=[
            pl.BlockSpec((TILES, rows, 128), lambda i: (0, i, 0)),
            pl.BlockSpec((TILES, rows, 128), lambda i: (0, i, 0)),
            whole((TILES, CHUNKS * STATE, 128)), whole((TILES, CHUNKS, 128)),
        ],
        out_shape=[
            jax.ShapeDtypeStruct((TILES, CLEN * CHUNKS, 128), f32),
            jax.ShapeDtypeStruct((TILES, CLEN * CHUNKS, 128), f32),
            jax.ShapeDtypeStruct((TILES, CHUNKS * STATE, 128), f32),
            jax.ShapeDtypeStruct((TILES, CHUNKS, 128), f32),
        ],
        scratch_shapes=[
            pltpu.VMEM((TILES, rows, 128), f32), pltpu.VMEM((TILES, rows, 128), f32),
            pltpu.VMEM((TILES, rows, 128), f32), pltpu.VMEM((rows, 2 * STATE * 128), f32),
            pltpu.VMEM((CHUNKS, 8, COLS), f32), pltpu.VMEM((TILES, STATE, CHUNKS, 128), f32),
            pltpu.VMEM((TILES, CHUNKS, 128), f32),
        ],
        compiler_params=pltpu.CompilerParams(vmem_limit_bytes=VMEM_LIMIT),
        cost_estimate=pl.CostEstimate(flops=100_000_000_000, bytes_accessed=16 * 2**20, transcendentals=0),
        name="scan_chunks",
    )(x, prior, low, mix, spread, w, convw, convb, bias, rate, skip)


def finish_kernel(y_ref, cum_ref, mix_ref, spread_ref, gate_ref, rate_ref, start_ref, out_ref, splat_s, ready_s):
    splat_s[...] = jnp.dot(mix_ref[...], spread_ref[...], preferred_element_type=jnp.float32)

    for j in range(TILES):
        cols = slice(j * 128, (j + 1) * 128)
        rates = [jnp.broadcast_to(rate_ref[n : n + 1, cols], (CHUNKS, 128)) for n in range(STATE)]
        starts = [start_ref.at[j][pl.ds(n, CHUNKS, stride=STATE), :] for n in range(STATE)]

        def correct(t, carry):
            rows = pl.ds(pl.multiple_of(t * CHUNKS, CHUNKS), CHUNKS)
            run = cum_ref[j, rows, :]
            terms = [
                jnp.exp2(run * rates[n]) * starts[n] * splat_s[rows, n * 128 : (n + 1) * 128]
                for n in range(STATE)
            ]
            ready_s[j, rows, :] = tree_sum(terms) + y_ref[j, rows, :]
            return carry

        lax.fori_loop(0, TB, correct, 0, unroll=8)

    def gate_chunk(chunk, carry):
        for j in range(TILES):
            cols = slice(j * 128, (j + 1) * 128)
            ssm = ready_s.at[j][pl.ds(chunk, TB, stride=CHUNKS), :].astype(jnp.bfloat16).astype(jnp.float32)
            gate = gate_ref[chunk, :, cols].astype(jnp.float32)
            out_ref[chunk, :, cols] = (ssm * (gate * jax.nn.sigmoid(gate))).astype(jnp.bfloat16)
        return carry

    lax.fori_loop(0, CHUNKS, gate_chunk, 0)


def finish_call(y, cum, mix_out, spread, gate, rate, starts):
    f32 = jnp.float32
    whole = lambda shape: pl.BlockSpec(shape, lambda i: (0,) * len(shape))
    rows = TB * CHUNKS
    tiles = pl.BlockSpec((TILES, rows, 128), lambda i: (0, i, 0))
    tokens = pl.BlockSpec((CHUNKS, TB, COLS), lambda i: (0, i, 0))
    return pl.pallas_call(
        finish_kernel,
        grid=(STEPS,),
        in_specs=[
            tiles, tiles, pl.BlockSpec((rows, STATE), lambda i: (i, 0)), whole((STATE, STATE * 128)), tokens,
            whole((STATE, COLS)), whole((TILES, CHUNKS * STATE, 128)),
        ],
        out_specs=tokens,
        out_shape=jax.ShapeDtypeStruct((CHUNKS, CLEN, COLS), jnp.bfloat16),
        scratch_shapes=[pltpu.VMEM((rows, STATE * 128), f32), pltpu.VMEM((TILES, rows, 128), f32)],
        compiler_params=pltpu.CompilerParams(vmem_limit_bytes=VMEM_LIMIT),
        cost_estimate=pl.CostEstimate(flops=50_000_000_000, bytes_accessed=16 * 2**20, transcendentals=0),
        name="finish_chunks",
    )(y, cum, mix_out, spread, gate, rate, starts)


QB = 512


def attention_kernel(side_ref, dev_ref, half_ref, diag_ref, first_ref, q_ref, kv_ref, o_ref, top_s, sum_s, acc_s):
    item = pl.program_id(0)
    scale = HD ** (-0.5) * LOG2E

    @pl.when(first_ref[item] == 1)
    def _():
        top_s[...] = jnp.full_like(top_s, NEG_LARGE)
        sum_s[...] = jnp.zeros_like(sum_s)
        acc_s[...] = jnp.zeros_like(acc_s)

    def absorb(masked):
        keys = kv_ref[0, :, 0, :, :HD].reshape(SPAN, HD)
        values = kv_ref[0, :, 0, :, HD:].reshape(SPAN, HD)
        for i in range(SPAN // QB):
            rows = slice(i * QB, (i + 1) * QB)
            scores = lax.dot_general(
                q_ref[0, rows, :], keys, (((1,), (1,)), ((), ())), preferred_element_type=jnp.float32
            ) * scale
            if masked:
                place = lax.broadcasted_iota(jnp.int32, (QB, SPAN), 1)
                key_pos = ((place // 64) % 4) * 256 + (place // 256) * 64 + place % 64
                query_pos = i * QB + lax.broadcasted_iota(jnp.int32, (QB, SPAN), 0)
                scores = jnp.where(key_pos <= query_pos, scores, NEG_LARGE)
            top = top_s[rows, :]
            new_top = jnp.maximum(top, jnp.max(scores, axis=1, keepdims=True))
            weights = jnp.exp2(scores - new_top[:, :1])
            shrink = jnp.exp2(top - new_top)
            top_s[rows, :] = new_top
            sum_s[rows, :] = sum_s[rows, :] * shrink + jnp.sum(weights, axis=1, keepdims=True)
            acc_s[rows, :] = acc_s[rows, :] * shrink + jnp.dot(
                weights.astype(jnp.bfloat16), values, preferred_element_type=jnp.float32
            )

    @pl.when(diag_ref[item] == 0)
    def _():
        absorb(False)

    @pl.when(diag_ref[item] == 1)
    def _():
        absorb(True)
        o_ref[0] = (acc_s[...] / sum_s[...]).astype(jnp.bfloat16)


def attention_call(side, dev, half, diag, first, q, kv):
    f32 = jnp.float32
    return pl.pallas_call(
        attention_kernel,
        grid_spec=pltpu.PrefetchScalarGridSpec(
            num_scalar_prefetch=5,
            grid=(17,),
            in_specs=[
                pl.BlockSpec((1, SPAN, HD), lambda i, side, dev, half, diag, first: (side[i], 0, 0)),
                pl.BlockSpec(
                    (1, 4, 1, 256, 2 * HD), lambda i, side, dev, half, diag, first: (dev[i], 0, half[i], 0, 0)
                ),
            ],
            out_specs=pl.BlockSpec((1, SPAN, HD), lambda i, side, dev, half, diag, first: (side[i], 0, 0)),
            scratch_shapes=[pltpu.VMEM((SPAN, 128), f32), pltpu.VMEM((SPAN, 128), f32), pltpu.VMEM((SPAN, HD), f32)],
        ),
        out_shape=jax.ShapeDtypeStruct((2, SPAN, HD), jnp.bfloat16),
        compiler_params=pltpu.CompilerParams(vmem_limit_bytes=VMEM_LIMIT),
        cost_estimate=pl.CostEstimate(flops=60_000_000_000, bytes_accessed=16 * 2**20, transcendentals=0),
        name="attend",
    )(side, dev, half, diag, first, q, kv)


WIDE = 640
TAIL = 16
MESH = pl.DeviceIdType.MESH


def intake_kernel(
    x_ref, low_ref, kv_ref, weight_ref, params_ref, x_out, low_out, tail_out, kv_out, weight_out, params_out, weight_mid, params_mid,
    own_sem, kv_send, kv_recv, swap_send, swap_recv, x_send, x_recv, low_send, low_recv, col_send, col_recv, tail_send, tail_recv,
):
    blk, z, w = lax.axis_index("blk"), lax.axis_index("z"), lax.axis_index("w")
    me = blk * 4 + w
    barrier = pltpu.get_barrier_semaphore()

    def greet(k, carry):
        peer = lax.rem(me + k, 32)
        pl.semaphore_signal(barrier, inc=1, device_id=(peer // 4, z, lax.rem(peer, 4)), device_id_type=MESH)
        return carry

    def greet_z(k, carry):
        pl.semaphore_signal(barrier, inc=1, device_id=(blk, lax.rem(z + k, 8), w), device_id_type=MESH)
        return carry

    lax.fori_loop(1, 32, greet, 0)
    lax.fori_loop(1, 8, greet_z, 0)

    pl.semaphore_wait(barrier, 38)

    def kv_copy(k):
        peer = lax.rem(z + k, 8)
        return pltpu.make_async_remote_copy(
            src_ref=kv_ref.at[:, pl.ds(pl.multiple_of(peer * 2 * HD, 2 * HD), 2 * HD)], dst_ref=kv_out.at[z],
            send_sem=kv_send.at[k], recv_sem=kv_recv.at[z], device_id=(blk, peer, w), device_id_type=MESH,
        )

    shift = lax.rem(blk - z + 8, 8)
    held, middle, settled = (weight_ref, params_ref), (weight_mid, params_mid), (weight_out, params_out)

    def along(slot):
        return pltpu.make_async_remote_copy(
            src_ref=held[slot], dst_ref=middle[slot], send_sem=swap_send.at[slot], recv_sem=swap_recv.at[slot],
            device_id=(blk, shift, w), device_id_type=MESH,
        )

    def along_here(slot):
        return pltpu.make_async_copy(held[slot], middle[slot], swap_recv.at[slot])

    def across_plane(slot):
        return pltpu.make_async_remote_copy(
            src_ref=middle[slot], dst_ref=settled[slot], send_sem=swap_send.at[2 + slot],
            recv_sem=swap_recv.at[2 + slot], device_id=(shift, z, w), device_id_type=MESH,
        )

    def across_here(slot):
        return pltpu.make_async_copy(middle[slot], settled[slot], swap_recv.at[2 + slot])

    def low_copy(k):
        return pltpu.make_async_remote_copy(
            src_ref=low_ref, dst_ref=low_out.at[blk, w], send_sem=low_send.at[k], recv_sem=low_recv.at[blk],
            device_id=(lax.rem(blk + k, 8), z, w), device_id_type=MESH,
        )

    def x_copy(k):
        peer = lax.rem(me + 1 + lax.rem(k - 1 + 11 * me, 31), 32)
        return pltpu.make_async_remote_copy(
            src_ref=x_ref.at[:, pl.ds(pl.multiple_of(peer * COLS, COLS), COLS)], dst_ref=x_out.at[blk, w],
            send_sem=x_send.at[k], recv_sem=x_recv.at[me],
            device_id=(peer // 4, z, lax.rem(peer, 4)), device_id_type=MESH,
        )

    def x_arrival(source):
        return pltpu.make_async_remote_copy(
            src_ref=x_out.at[source // 4, lax.rem(source, 4)], dst_ref=x_out.at[source // 4, lax.rem(source, 4)],
            send_sem=x_send.at[0],
            recv_sem=x_recv.at[source], device_id=(blk, z, w), device_id_type=MESH,
        )

    def start(copy):
        def go(k, carry):
            copy(k).start()
            return carry

        return go

    own_low = pltpu.make_async_copy(low_ref, low_out.at[blk, w], own_sem.at[0])
    own_x = pltpu.make_async_copy(
        x_ref.at[:, pl.ds(pl.multiple_of(me * COLS, COLS), COLS)], x_out.at[blk, w], own_sem.at[1]
    )
    own_low.start()
    lax.fori_loop(1, 8, start(low_copy), 0)
    own_kv = pltpu.make_async_copy(
        kv_ref.at[:, pl.ds(pl.multiple_of(z * 2 * HD, 2 * HD), 2 * HD)], kv_out.at[z], own_sem.at[2]
    )

    @pl.when(shift != z)
    def _():
        along(0).start()
        along(1).start()

    @pl.when(shift == z)
    def _():
        along_here(0).start()
        along_here(1).start()

    own_x.start()
    own_kv.start()
    lax.fori_loop(1, 12, start(x_copy), 0)
    lax.fori_loop(1, 8, start(kv_copy), 0)

    def low_arrived(k, carry):
        source = lax.rem(blk + k, 8)
        pltpu.make_async_remote_copy(
            src_ref=low_out.at[source, w], dst_ref=low_out.at[source, w], send_sem=low_send.at[0],
            recv_sem=low_recv.at[source], device_id=(blk, z, w), device_id_type=MESH,
        ).wait_recv()
        return carry

    own_low.wait()
    lax.fori_loop(1, 8, low_arrived, 0)
    across = lax.rem(w + 2, 4)
    sibling = (w // 2) * 2 + 1 - lax.rem(w, 2)
    sibling_across = lax.rem(sibling + 2, 4)

    def column(which, slot, target):
        return pltpu.make_async_remote_copy(
            src_ref=low_out.at[:, which], dst_ref=low_out.at[:, which], send_sem=col_send.at[slot],
            recv_sem=col_recv.at[slot], device_id=(blk, z, target), device_id_type=MESH,
        )

    over = column(w, 0, across)
    beside = column(w, 1, sibling)
    over.start()
    beside.start()
    lax.fori_loop(12, 32, start(x_copy), 0)

    @pl.when(shift != z)
    def _():
        for slot in range(2):
            along(slot).wait_recv()
            along(slot).wait_send()

    @pl.when(shift == z)
    def _():
        along_here(0).wait()
        along_here(1).wait()

    @pl.when(z != 0)
    def _():
        across_plane(0).start()
        across_plane(1).start()

    @pl.when(z == 0)
    def _():
        across_here(0).start()
        across_here(1).start()
    column(across, 0, across).wait_recv()
    relay = column(across, 2, sibling)
    relay.start()

    own_x.wait()

    def wait_x(k, carry):
        x_arrival(lax.rem(me + k, 32)).wait_recv()
        return carry

    lax.fori_loop(1, 32, wait_x, 0)

    part, quarter = z // 4, lax.rem(z, 4)

    def tail_copy(slot, which, target):
        return pltpu.make_async_remote_copy(
            src_ref=x_out.at[:, 3, pl.ds(64 - TAIL, TAIL)], dst_ref=tail_out.at[slot],
            send_sem=tail_send.at[which], recv_sem=tail_recv.at[slot],
            device_id=(blk, target, w), device_id_type=MESH,
        )

    @pl.when(quarter != 3)
    def _():
        tail_copy(0, 0, lax.rem(z + 1, 8)).start()

    @pl.when(quarter == 3)
    def _():
        tail_copy(part, 0, 0).start()
        tail_copy(part, 1, 4).start()

    column(sibling, 1, sibling).wait_recv()
    column(sibling_across, 2, sibling).wait_recv()

    @pl.when(quarter != 0)
    def _():
        tail_copy(0, 0, lax.rem(z + 1, 8)).wait_recv()

    @pl.when(quarter == 0)
    def _():
        tail_copy(0, 0, lax.rem(z + 1, 8)).wait_recv()
        tail_copy(1, 0, lax.rem(z + 1, 8)).wait_recv()

    tail_copy(0, 0, lax.rem(z + 1, 8)).wait_send()

    @pl.when(quarter == 3)
    def _():
        tail_copy(0, 1, lax.rem(z + 1, 8)).wait_send()

    def low_sent(k, carry):
        low_copy(k).wait_send()
        return carry

    def x_sent(k, carry):
        x_copy(k).wait_send()
        return carry

    own_kv.wait()

    def kv_done(k, carry):
        source = lax.rem(z + k, 8)
        pltpu.make_async_remote_copy(
            src_ref=kv_out.at[source], dst_ref=kv_out.at[source], send_sem=kv_send.at[0],
            recv_sem=kv_recv.at[source], device_id=(blk, z, w), device_id_type=MESH,
        ).wait_recv()
        kv_copy(k).wait_send()
        return carry

    lax.fori_loop(1, 8, kv_done, 0)

    @pl.when(z != 0)
    def _():
        for slot in range(2):
            across_plane(slot).wait_recv()
            across_plane(slot).wait_send()

    @pl.when(z == 0)
    def _():
        across_here(0).wait()
        across_here(1).wait()

    lax.fori_loop(1, 8, low_sent, 0)
    lax.fori_loop(1, 32, x_sent, 0)
    over.wait_send()
    beside.wait_send()
    relay.wait_send()


def intake_call(x, low, kv, weight, params):
    anywhere = pl.BlockSpec(memory_space=pl.ANY)
    sems = pltpu.SemaphoreType.DMA
    return pl.pallas_call(
        intake_kernel,
        in_specs=[anywhere] * 5,
        out_specs=[anywhere] * 8,
        out_shape=[
            jax.ShapeDtypeStruct((8, 4, 64, COLS), jnp.bfloat16),
            jax.ShapeDtypeStruct((8, 4, 64, WIDE), jnp.bfloat16),
            jax.ShapeDtypeStruct((2, 8, TAIL, COLS), jnp.bfloat16),
            jax.ShapeDtypeStruct((8, 64, 2 * HD), jnp.bfloat16),
            jax.ShapeDtypeStruct(weight.shape, weight.dtype),
            jax.ShapeDtypeStruct(params.shape, params.dtype),
            jax.ShapeDtypeStruct(weight.shape, weight.dtype),
            jax.ShapeDtypeStruct(params.shape, params.dtype),
        ],
        scratch_shapes=[
            sems((3,)), sems((8,)), sems((8,)), sems((4,)), sems((4,)), sems((32,)), sems((32,)), sems((8,)), sems((8,)),
            sems((3,)), sems((3,)),
            sems((2,)), sems((2,)),
        ],
        compiler_params=pltpu.CompilerParams(collective_id=0, has_side_effects=True),
        name="intake",
    )(x, low, kv, weight, params)


def states_kernel(
    order_ref, end_ref, sum_ref, rate_ref, start_ref,
    got_end, got_sum, chain, reply, own_sem, end_send, end_recv, sum_send, sum_recv, back_send, back_recv,
):
    blk, z, w = lax.axis_index("blk"), lax.axis_index("z"), lax.axis_index("w")
    barrier = pltpu.get_barrier_semaphore()

    def greet(k, carry):
        pl.semaphore_signal(barrier, inc=1, device_id=(blk, lax.rem(z + k, 8), w), device_id_type=MESH)
        return carry

    lax.fori_loop(1, 8, greet, 0)
    pl.semaphore_wait(barrier, 7)
    mine = pl.ds(pl.multiple_of(z * 8, 8), 8)

    def remote(src, dst, send, recv, target):
        return pltpu.make_async_remote_copy(
            src_ref=src, dst_ref=dst, send_sem=send, recv_sem=recv, device_id=(blk, target, w), device_id_type=MESH
        )

    def end_copy(k):
        peer = lax.rem(z + k, 8)
        return remote(
            end_ref.at[peer // 2, :, lax.rem(peer, 2)], got_end.at[mine], end_send.at[k], end_recv.at[z], peer
        )

    def sum_copy(k):
        peer = lax.rem(z + k, 8)
        return remote(sum_ref.at[peer // 2], got_sum.at[mine], sum_send.at[k], sum_recv.at[z], peer)

    def back_copy(k):
        peer = lax.rem(z + k, 8)
        return remote(
            reply.at[pl.ds(pl.multiple_of(peer * 8, 8), 8)], start_ref.at[z // 2, :, lax.rem(z, 2)],
            back_send.at[k], back_recv.at[z], peer,
        )

    def send_ends(k, carry):
        end_copy(k).start()
        sum_copy(k).start()
        return carry

    lax.fori_loop(1, 8, send_ends, 0)
    own_end = pltpu.make_async_copy(end_ref.at[z // 2, :, lax.rem(z, 2)], got_end.at[mine], own_sem.at[0])
    own_sum = pltpu.make_async_copy(sum_ref.at[z // 2], got_sum.at[mine], own_sem.at[1])
    own_end.start()
    own_sum.start()
    own_end.wait()
    own_sum.wait()

    def ends_arrived(k, carry):
        source = lax.rem(z + k, 8)
        there = pl.ds(pl.multiple_of(source * 8, 8), 8)
        remote(got_end.at[there], got_end.at[there], end_send.at[0], end_recv.at[source], z).wait_recv()
        remote(got_sum.at[there], got_sum.at[there], sum_send.at[0], sum_recv.at[source], z).wait_recv()
        return carry

    lax.fori_loop(1, 8, ends_arrived, 0)
    rate = rate_ref[z // 2, lax.rem(z, 2)]

    def carry_on(position, state):
        chain[position] = state
        index = order_ref[position]
        return jnp.exp2(rate * got_sum[pl.ds(index, 1), :]) * state + got_end[index]

    lax.fori_loop(0, 64, carry_on, jnp.zeros((8, 128), jnp.float32))

    def pick(index, carry):
        reply[index] = chain[order_ref[64 + index]]
        return carry

    lax.fori_loop(0, 64, pick, 0)

    def send_back(k, carry):
        back_copy(k).start()
        return carry

    lax.fori_loop(1, 8, send_back, 0)
    own_back = pltpu.make_async_copy(reply.at[mine], start_ref.at[z // 2, :, lax.rem(z, 2)], own_sem.at[2])
    own_back.start()
    own_back.wait()

    def finish(k, carry):
        source = lax.rem(z + k, 8)
        landed = start_ref.at[source // 2, :, lax.rem(source, 2)]
        remote(landed, landed, back_send.at[0], back_recv.at[source], z).wait_recv()
        end_copy(k).wait_send()
        sum_copy(k).wait_send()
        back_copy(k).wait_send()
        return carry

    lax.fori_loop(1, 8, finish, 0)


def states_call(order, ends, sums, rate):
    f32 = jnp.float32
    here = pl.BlockSpec(memory_space=pltpu.VMEM)
    sems = pltpu.SemaphoreType.DMA
    return pl.pallas_call(
        states_kernel,
        in_specs=[pl.BlockSpec(memory_space=pltpu.SMEM), here, here, here],
        out_specs=here,
        out_shape=jax.ShapeDtypeStruct((TILES, CHUNKS, 2, 8, 128), f32),
        scratch_shapes=[
            pltpu.VMEM((64, 8, 128), f32), pltpu.VMEM((64, 128), f32), pltpu.VMEM((64, 8, 128), f32),
            pltpu.VMEM((64, 8, 128), f32), sems((3,)), sems((8,)), sems((8,)), sems((8,)), sems((8,)),
            sems((8,)), sems((8,)),
        ],
        compiler_params=pltpu.CompilerParams(collective_id=1, has_side_effects=True),
        name="chain_states",
    )(order, ends, sums, rate)


ULYS = ("z", "w")
PLANE = ("blk", "w")


def local(
    mamba_input, gate_input, delta_low, state_mixers, conv_weight, conv_bias, delta_weight, delta_bias,
    decay_log, skip_gain, queries, key_rows, value_rows, span_order,
):
    f32 = jnp.float32
    me, z = lax.axis_index("blk"), lax.axis_index("z")
    zpart = z // 4
    params = jnp.concatenate(
        [
            -jnp.exp(decay_log) * LOG2E, conv_weight.astype(f32), conv_bias[None, :], delta_bias[None, :],
            skip_gain[None, :], jnp.zeros((1, COLS), f32),
        ],
        axis=0,
    )
    places = jnp.arange(16, dtype=jnp.int32)
    mine = lax.dynamic_slice_in_dim(span_order, 2 * me, 2, 0)

    low_mix = jnp.concatenate(
        [delta_low, state_mixers, jnp.zeros((64, WIDE - 512 - 2 * STATE), jnp.bfloat16)], axis=1
    )
    kv = jnp.concatenate([key_rows.reshape(64, 8, HD), value_rows.reshape(64, 8, HD)], axis=2)
    x, low_mix, tails, kv, weight, params, _, _ = intake_call(
        mamba_input, low_mix, kv.reshape(64, 8 * 2 * HD), delta_weight, params
    )
    x, gate_input, queries = lax.optimization_barrier((x, gate_input, queries))
    rate = params[:STATE]
    low = low_mix.reshape(CHUNKS, CLEN, WIDE)
    mix = (
        low[:, :, 512 : 512 + 2 * STATE].swapaxes(0, 1).reshape(CHUNKS * CLEN, 2 * STATE)
    )
    x = x.reshape(CHUNKS, CLEN, COLS)
    places = places[:, None]
    earlier = span_order.reshape(CHUNKS, 2)[:, zpart] - 1
    follows = (earlier[:, None] == span_order[None, :]).astype(jnp.bfloat16)
    at_start = lax.rem(z, 4) == 0
    tails = tails[:, :, TAIL - 8 :]
    of_block = tails.swapaxes(0, 1).reshape(16, 8, COLS)
    before = jnp.einsum("cj,jtk->ctk", follows, of_block, preferred_element_type=f32)
    prior = jnp.where(at_start, before, tails[0].astype(f32))
    spread = jnp.repeat(jnp.eye(2 * STATE, dtype=jnp.bfloat16), 128, axis=1)

    y, cum, end, sums = scan_call(
        x, prior, low, mix, spread, weight, params[16:20], params[20:21], params[21:22], rate, params[22:23],
    )

    gate = lax.all_to_all(gate_input, PLANE, split_axis=1, concat_axis=0, tiled=True)
    query = lax.all_to_all(queries, ULYS, split_axis=1, concat_axis=0, tiled=True)
    kv = lax.all_gather(kv.reshape(512, 2 * HD), PLANE, axis=0, tiled=True).reshape(8, 4, 2, 256, 2 * HD)

    items = jnp.arange(17, dtype=jnp.int32)
    second = (items > mine[0]).astype(jnp.int32)
    place = jnp.where(second == 1, items - mine[0] - 1, items)
    stored = jnp.sum(jnp.where(place[:, None] == span_order[None, :], places.T, 0), axis=1)
    diag = (place == jnp.where(second == 1, mine[1], mine[0])).astype(jnp.int32)
    first = (place == 0).astype(jnp.int32)
    attended = attention_call(
        second, stored // 2, stored % 2, diag, first, query.reshape(2, SPAN, HD), kv
    ).reshape(2 * SPAN, HD)

    steps = jnp.arange(64, dtype=jnp.int32)
    at = jnp.sum(jnp.where((steps // 4)[:, None] == span_order[None, :], places.T, 0), axis=1)
    index_of = ((at % 2) * 4 + steps % 4) * 8 + at // 2
    block_of = 2 * (steps % 8) + steps // 32
    place_of = jnp.sum(jnp.where(block_of[:, None] == places.T, span_order[None, :], 0), axis=1)
    position_of = place_of * 4 + (steps // 8) % 4
    starts = states_call(
        jnp.concatenate([index_of, position_of]), end.reshape(TILES, CHUNKS, 2, 8, 128), sums,
        rate.reshape(2, 8, TILES, 128).transpose(2, 0, 1, 3),
    )
    gated = finish_call(
        y, cum, mix[:, STATE:], spread[:STATE, : STATE * 128], gate.reshape(CHUNKS, CLEN, COLS), rate,
        starts.reshape(TILES, CHUNKS * STATE, 128),
    ).reshape(CHUNKS * CLEN, COLS)
    mamba_output = lax.all_to_all(gated, PLANE, split_axis=0, concat_axis=1, tiled=True)
    attention_output = lax.all_to_all(attended, ULYS, split_axis=0, concat_axis=1, tiled=True)
    return (mamba_output, attention_output)


def solution(mesh):
    tokens = P(("blk", "z", "w"), None)
    wide = P(None, ULYS)
    flat = P(ULYS)
    placed = (
        tokens, tokens, tokens, tokens, wide, flat, wide, flat, wide, flat, tokens, tokens, tokens, P(),
    )
    split_mesh = Mesh(mesh.devices.reshape(8, 8, 4), ("blk", "z", "w"))
    return jax.shard_map(
        local, mesh=split_mesh, in_specs=placed, out_specs=(tokens, tokens), check_vma=False
    )
```

```python
import functools

import jax
import jax.numpy as jnp
from jax import lax
from jax.experimental import pallas as pl
from jax.experimental.pallas import tpu as pltpu
from jax.sharding import Mesh, PartitionSpec as P

STATE = 16
CONV = 4
HD = 128
SPAN = 1024
CHUNKS = 8
CLEN = 256
COLS = 512
TILES = COLS // 128
TB = 32
STEPS = CLEN // TB
NEG_LARGE = -1e30
LOG2E = 1.4426950408889634
VMEM_LIMIT = 56 * 2**20


def tree_sum(terms):
    while len(terms) > 1:
        terms = [a + b for a, b in zip(terms[::2], terms[1::2])] + terms[len(terms) // 2 * 2 :]
    return terms[0]


def scan_kernel(
    x_ref, prior_ref, low_ref, mix_ref, spread_ref, w_ref, convw_ref, convb_ref, bias_ref, rate_ref, skip_ref,
    y_ref, cum_ref, end_ref, sum_ref,
    delta_s, dx_s, direct_s, splat_s, tail_s, state_s, run_s, raw_s,
):
    step = pl.program_id(0)

    @pl.when(step == 0)
    def _():
        tail_s[...] = prior_ref[...]
        state_s[...] = jnp.zeros_like(state_s)
        run_s[...] = jnp.zeros_like(run_s)

    splat_s[...] = jnp.dot(mix_ref[...], spread_ref[...], preferred_element_type=jnp.float32)

    raw_s[...] = jnp.dot(
        low_ref[...].reshape(CHUNKS * TB, 512), w_ref[...], preferred_element_type=jnp.float32
    )

    def prepare(chunk, carry):
        x = x_ref[chunk].astype(jnp.float32)
        padded = jnp.concatenate([tail_s[chunk], x], axis=0)
        mixed = convb_ref[...] + convw_ref[CONV - 1 : CONV, :] * x
        for k in range(CONV - 1):
            mixed = mixed + convw_ref[k : k + 1, :] * padded[8 - (CONV - 1) + k : 8 - (CONV - 1) + k + TB]
        tail_s[chunk] = x[TB - 8 :]
        driven = mixed * jax.nn.sigmoid(mixed)
        raw = raw_s[pl.ds(pl.multiple_of(chunk * TB, TB), TB), :] + bias_ref[...]
        delta = jnp.maximum(raw, 0.0) + jnp.log1p(jnp.exp(-jnp.abs(raw)))
        dx = delta * driven
        direct = skip_ref[...] * driven
        for j in range(TILES):
            cols = slice(j * 128, (j + 1) * 128)
            rows = pl.ds(chunk, TB, stride=CHUNKS)
            delta_s.at[j][rows, :] = delta[:, cols]
            dx_s.at[j][rows, :] = dx[:, cols]
            direct_s.at[j][rows, :] = direct[:, cols]
        return carry

    lax.fori_loop(0, CHUNKS, prepare, 0)

    for j in range(TILES):
        cols = slice(j * 128, (j + 1) * 128)
        rates = [jnp.broadcast_to(rate_ref[n : n + 1, cols], (CHUNKS, 128)) for n in range(STATE)]

        def advance(t, carry):
            hidden, run = carry
            rows = pl.ds(pl.multiple_of(t * CHUNKS, CHUNKS), CHUNKS)
            delta = delta_s[j, rows, :]
            dx = dx_s[j, rows, :]
            hidden = tuple(
                jnp.exp2(delta * rates[n]) * hidden[n] + dx * splat_s[rows, n * 128 : (n + 1) * 128]
                for n in range(STATE)
            )
            terms = [
                hidden[n] * splat_s[rows, (STATE + n) * 128 : (STATE + n + 1) * 128] for n in range(STATE)
            ]
            run = run + delta
            y_ref[j, rows, :] = tree_sum(terms) + direct_s[j, rows, :]
            cum_ref[j, rows, :] = run
            return (hidden, run)

        hidden, run = lax.fori_loop(
            0, TB, advance, (tuple(state_s[j, n] for n in range(STATE)), run_s[j]), unroll=8
        )
        for n in range(STATE):
            state_s[j, n] = hidden[n]
        run_s[j] = run

    @pl.when(step == STEPS - 1)
    def _():
        for j in range(TILES):
            for n in range(STATE):
                end_ref.at[j][pl.ds(n, CHUNKS, stride=STATE), :] = state_s[j, n]
            sum_ref[j] = run_s[j]


def scan_call(x, prior, low, mix, spread, w, convw, convb, bias, rate, skip):
    f32 = jnp.float32
    whole = lambda shape: pl.BlockSpec(shape, lambda i: (0,) * len(shape))
    tokens = lambda width: pl.BlockSpec((CHUNKS, TB, width), lambda i: (0, i, 0))
    rows = TB * CHUNKS
    return pl.pallas_call(
        scan_kernel,
        grid=(STEPS,),
        in_specs=[
            tokens(COLS), whole((CHUNKS, 8, COLS)), tokens(512),
            pl.BlockSpec((rows, 2 * STATE), lambda i: (i, 0)), whole((2 * STATE, 2 * STATE * 128)),
            whole((512, COLS)), whole((CONV, COLS)), whole((1, COLS)), whole((1, COLS)),
            whole((STATE, COLS)), whole((1, COLS)),
        ],
        out_specs=[
            pl.BlockSpec((TILES, rows, 128), lambda i: (0, i, 0)),
            pl.BlockSpec((TILES, rows, 128), lambda i: (0, i, 0)),
            whole((TILES, CHUNKS * STATE, 128)), whole((TILES, CHUNKS, 128)),
        ],
        out_shape=[
            jax.ShapeDtypeStruct((TILES, CLEN * CHUNKS, 128), f32),
            jax.ShapeDtypeStruct((TILES, CLEN * CHUNKS, 128), f32),
            jax.ShapeDtypeStruct((TILES, CHUNKS * STATE, 128), f32),
            jax.ShapeDtypeStruct((TILES, CHUNKS, 128), f32),
        ],
        scratch_shapes=[
            pltpu.VMEM((TILES, rows, 128), f32), pltpu.VMEM((TILES, rows, 128), f32),
            pltpu.VMEM((TILES, rows, 128), f32), pltpu.VMEM((rows, 2 * STATE * 128), f32),
            pltpu.VMEM((CHUNKS, 8, COLS), f32), pltpu.VMEM((TILES, STATE, CHUNKS, 128), f32),
            pltpu.VMEM((TILES, CHUNKS, 128), f32), pltpu.VMEM((rows, COLS), f32),
        ],
        compiler_params=pltpu.CompilerParams(vmem_limit_bytes=VMEM_LIMIT),
        cost_estimate=pl.CostEstimate(flops=100_000_000_000, bytes_accessed=16 * 2**20, transcendentals=0),
        name="scan_chunks",
    )(x, prior, low, mix, spread, w, convw, convb, bias, rate, skip)


def finish_kernel(y_ref, cum_ref, mix_ref, spread_ref, gate_ref, rate_ref, start_ref, out_ref, splat_s, ready_s):
    splat_s[...] = jnp.dot(mix_ref[...], spread_ref[...], preferred_element_type=jnp.float32)

    for j in range(TILES):
        cols = slice(j * 128, (j + 1) * 128)
        rates = [jnp.broadcast_to(rate_ref[n : n + 1, cols], (CHUNKS, 128)) for n in range(STATE)]
        starts = [start_ref.at[j][pl.ds(n, CHUNKS, stride=STATE), :] for n in range(STATE)]

        def correct(t, carry):
            rows = pl.ds(pl.multiple_of(t * CHUNKS, CHUNKS), CHUNKS)
            run = cum_ref[j, rows, :]
            terms = [
                jnp.exp2(run * rates[n]) * starts[n] * splat_s[rows, n * 128 : (n + 1) * 128]
                for n in range(STATE)
            ]
            ready_s[j, rows, :] = tree_sum(terms) + y_ref[j, rows, :]
            return carry

        lax.fori_loop(0, TB, correct, 0, unroll=8)

    def gate_chunk(chunk, carry):
        for j in range(TILES):
            cols = slice(j * 128, (j + 1) * 128)
            ssm = ready_s.at[j][pl.ds(chunk, TB, stride=CHUNKS), :].astype(jnp.bfloat16).astype(jnp.float32)
            gate = gate_ref[chunk, :, cols].astype(jnp.float32)
            out_ref[chunk, :, cols] = (ssm * (gate * jax.nn.sigmoid(gate))).astype(jnp.bfloat16)
        return carry

    lax.fori_loop(0, CHUNKS, gate_chunk, 0)


def finish_call(y, cum, mix_out, spread, gate, rate, starts):
    f32 = jnp.float32
    whole = lambda shape: pl.BlockSpec(shape, lambda i: (0,) * len(shape))
    rows = TB * CHUNKS
    tiles = pl.BlockSpec((TILES, rows, 128), lambda i: (0, i, 0))
    tokens = pl.BlockSpec((CHUNKS, TB, COLS), lambda i: (0, i, 0))
    return pl.pallas_call(
        finish_kernel,
        grid=(STEPS,),
        in_specs=[
            tiles, tiles, pl.BlockSpec((rows, STATE), lambda i: (i, 0)), whole((STATE, STATE * 128)), tokens,
            whole((STATE, COLS)), whole((TILES, CHUNKS * STATE, 128)),
        ],
        out_specs=tokens,
        out_shape=jax.ShapeDtypeStruct((CHUNKS, CLEN, COLS), jnp.bfloat16),
        scratch_shapes=[pltpu.VMEM((rows, STATE * 128), f32), pltpu.VMEM((TILES, rows, 128), f32)],
        compiler_params=pltpu.CompilerParams(vmem_limit_bytes=VMEM_LIMIT),
        cost_estimate=pl.CostEstimate(flops=50_000_000_000, bytes_accessed=16 * 2**20, transcendentals=0),
        name="finish_chunks",
    )(y, cum, mix_out, spread, gate, rate, starts)


QB = 512


def attention_kernel(side_ref, dev_ref, half_ref, diag_ref, first_ref, q_ref, kv_ref, o_ref, top_s, sum_s, acc_s):
    item = pl.program_id(0)
    scale = HD ** (-0.5) * LOG2E

    @pl.when(first_ref[item] == 1)
    def _():
        top_s[...] = jnp.full_like(top_s, NEG_LARGE)
        sum_s[...] = jnp.zeros_like(sum_s)
        acc_s[...] = jnp.zeros_like(acc_s)

    def absorb(masked):
        keys = kv_ref[0, :, 0, :, :HD].reshape(SPAN, HD)
        values = kv_ref[0, :, 0, :, HD:].reshape(SPAN, HD)
        for i in range(SPAN // QB):
            rows = slice(i * QB, (i + 1) * QB)
            scores = lax.dot_general(
                q_ref[0, rows, :], keys, (((1,), (1,)), ((), ())), preferred_element_type=jnp.float32
            ) * scale
            if masked:
                place = lax.broadcasted_iota(jnp.int32, (QB, SPAN), 1)
                key_pos = ((place // 64) % 4) * 256 + (place // 256) * 64 + place % 64
                query_pos = i * QB + lax.broadcasted_iota(jnp.int32, (QB, SPAN), 0)
                scores = jnp.where(key_pos <= query_pos, scores, NEG_LARGE)
            top = top_s[rows, :]
            new_top = jnp.maximum(top, jnp.max(scores, axis=1, keepdims=True))
            weights = jnp.exp2(scores - new_top[:, :1])
            shrink = jnp.exp2(top - new_top)
            top_s[rows, :] = new_top
            sum_s[rows, :] = sum_s[rows, :] * shrink + jnp.sum(weights, axis=1, keepdims=True)
            acc_s[rows, :] = acc_s[rows, :] * shrink + jnp.dot(
                weights.astype(jnp.bfloat16), values, preferred_element_type=jnp.float32
            )

    @pl.when(diag_ref[item] == 0)
    def _():
        absorb(False)

    @pl.when(diag_ref[item] == 1)
    def _():
        absorb(True)
        o_ref[0] = (acc_s[...] / sum_s[...]).astype(jnp.bfloat16)


def attention_call(side, dev, half, diag, first, q, kv):
    f32 = jnp.float32
    return pl.pallas_call(
        attention_kernel,
        grid_spec=pltpu.PrefetchScalarGridSpec(
            num_scalar_prefetch=5,
            grid=(17,),
            in_specs=[
                pl.BlockSpec((1, SPAN, HD), lambda i, side, dev, half, diag, first: (side[i], 0, 0)),
                pl.BlockSpec(
                    (1, 4, 1, 256, 2 * HD), lambda i, side, dev, half, diag, first: (dev[i], 0, half[i], 0, 0)
                ),
            ],
            out_specs=pl.BlockSpec((1, SPAN, HD), lambda i, side, dev, half, diag, first: (side[i], 0, 0)),
            scratch_shapes=[pltpu.VMEM((SPAN, 128), f32), pltpu.VMEM((SPAN, 128), f32), pltpu.VMEM((SPAN, HD), f32)],
        ),
        out_shape=jax.ShapeDtypeStruct((2, SPAN, HD), jnp.bfloat16),
        compiler_params=pltpu.CompilerParams(vmem_limit_bytes=VMEM_LIMIT),
        cost_estimate=pl.CostEstimate(flops=60_000_000_000, bytes_accessed=16 * 2**20, transcendentals=0),
        name="attend",
    )(side, dev, half, diag, first, q, kv)


WIDE = 640
TAIL = 16
MESH = pl.DeviceIdType.MESH


def intake_kernel(
    x_ref, low_ref, kv_ref, weight_ref, params_ref, x_out, low_out, tail_out, kv_out, weight_out, params_out, weight_mid, params_mid,
    own_sem, kv_send, kv_recv, swap_send, swap_recv, x_send, x_recv, low_send, low_recv, col_send, col_recv, tail_send, tail_recv,
):
    blk, z, w = lax.axis_index("blk"), lax.axis_index("z"), lax.axis_index("w")
    me = blk * 4 + w
    barrier = pltpu.get_barrier_semaphore()

    def greet(k, carry):
        peer = lax.rem(me + k, 32)
        pl.semaphore_signal(barrier, inc=1, device_id=(peer // 4, z, lax.rem(peer, 4)), device_id_type=MESH)
        return carry

    def greet_z(k, carry):
        pl.semaphore_signal(barrier, inc=1, device_id=(blk, lax.rem(z + k, 8), w), device_id_type=MESH)
        return carry

    lax.fori_loop(1, 32, greet, 0)
    lax.fori_loop(1, 8, greet_z, 0)

    pl.semaphore_wait(barrier, 38)

    def kv_copy(k):
        peer = lax.rem(z + k, 8)
        return pltpu.make_async_remote_copy(
            src_ref=kv_ref.at[:, pl.ds(pl.multiple_of(peer * 2 * HD, 2 * HD), 2 * HD)], dst_ref=kv_out.at[z],
            send_sem=kv_send.at[k], recv_sem=kv_recv.at[z], device_id=(blk, peer, w), device_id_type=MESH,
        )

    shift = lax.rem(blk - z + 8, 8)
    held, middle, settled = (weight_ref, params_ref), (weight_mid, params_mid), (weight_out, params_out)

    def along(slot):
        return pltpu.make_async_remote_copy(
            src_ref=held[slot], dst_ref=middle[slot], send_sem=swap_send.at[slot], recv_sem=swap_recv.at[slot],
            device_id=(blk, shift, w), device_id_type=MESH,
        )

    def along_here(slot):
        return pltpu.make_async_copy(held[slot], middle[slot], swap_recv.at[slot])

    def across_plane(slot):
        return pltpu.make_async_remote_copy(
            src_ref=middle[slot], dst_ref=settled[slot], send_sem=swap_send.at[2 + slot],
            recv_sem=swap_recv.at[2 + slot], device_id=(shift, z, w), device_id_type=MESH,
        )

    def across_here(slot):
        return pltpu.make_async_copy(middle[slot], settled[slot], swap_recv.at[2 + slot])

    def low_copy(k):
        return pltpu.make_async_remote_copy(
            src_ref=low_ref, dst_ref=low_out.at[blk, w], send_sem=low_send.at[k], recv_sem=low_recv.at[blk],
            device_id=(lax.rem(blk + k, 8), z, w), device_id_type=MESH,
        )

    def x_copy(k):
        peer = lax.rem(me + 1 + lax.rem(k - 1 + 11 * me, 31), 32)
        return pltpu.make_async_remote_copy(
            src_ref=x_ref.at[:, pl.ds(pl.multiple_of(peer * COLS, COLS), COLS)], dst_ref=x_out.at[blk, w],
            send_sem=x_send.at[k], recv_sem=x_recv.at[me],
            device_id=(peer // 4, z, lax.rem(peer, 4)), device_id_type=MESH,
        )

    def x_arrival(source):
        return pltpu.make_async_remote_copy(
            src_ref=x_out.at[source // 4, lax.rem(source, 4)], dst_ref=x_out.at[source // 4, lax.rem(source, 4)],
            send_sem=x_send.at[0],
            recv_sem=x_recv.at[source], device_id=(blk, z, w), device_id_type=MESH,
        )

    def start(copy):
        def go(k, carry):
            copy(k).start()
            return carry

        return go

    own_low = pltpu.make_async_copy(low_ref, low_out.at[blk, w], own_sem.at[0])
    own_x = pltpu.make_async_copy(
        x_ref.at[:, pl.ds(pl.multiple_of(me * COLS, COLS), COLS)], x_out.at[blk, w], own_sem.at[1]
    )
    own_low.start()
    lax.fori_loop(1, 8, start(low_copy), 0)
    own_kv = pltpu.make_async_copy(
        kv_ref.at[:, pl.ds(pl.multiple_of(z * 2 * HD, 2 * HD), 2 * HD)], kv_out.at[z], own_sem.at[2]
    )

    @pl.when(shift != z)
    def _():
        along(0).start()
        along(1).start()

    @pl.when(shift == z)
    def _():
        along_here(0).start()
        along_here(1).start()

    own_x.start()
    own_kv.start()
    lax.fori_loop(1, 12, start(x_copy), 0)
    lax.fori_loop(1, 8, start(kv_copy), 0)

    def low_arrived(k, carry):
        source = lax.rem(blk + k, 8)
        pltpu.make_async_remote_copy(
            src_ref=low_out.at[source, w], dst_ref=low_out.at[source, w], send_sem=low_send.at[0],
            recv_sem=low_recv.at[source], device_id=(blk, z, w), device_id_type=MESH,
        ).wait_recv()
        return carry

    own_low.wait()
    lax.fori_loop(1, 8, low_arrived, 0)
    across = lax.rem(w + 2, 4)
    sibling = (w // 2) * 2 + 1 - lax.rem(w, 2)
    sibling_across = lax.rem(sibling + 2, 4)

    def column(which, slot, target):
        return pltpu.make_async_remote_copy(
            src_ref=low_out.at[:, which], dst_ref=low_out.at[:, which], send_sem=col_send.at[slot],
            recv_sem=col_recv.at[slot], device_id=(blk, z, target), device_id_type=MESH,
        )

    over = column(w, 0, across)
    beside = column(w, 1, sibling)
    over.start()
    beside.start()
    lax.fori_loop(12, 32, start(x_copy), 0)

    @pl.when(shift != z)
    def _():
        for slot in range(2):
            along(slot).wait_recv()
            along(slot).wait_send()

    @pl.when(shift == z)
    def _():
        along_here(0).wait()
        along_here(1).wait()

    @pl.when(z != 0)
    def _():
        across_plane(0).start()
        across_plane(1).start()

    @pl.when(z == 0)
    def _():
        across_here(0).start()
        across_here(1).start()
    column(across, 0, across).wait_recv()
    relay = column(across, 2, sibling)
    relay.start()

    own_x.wait()

    def wait_x(k, carry):
        x_arrival(lax.rem(me + k, 32)).wait_recv()
        return carry

    lax.fori_loop(1, 32, wait_x, 0)

    part, quarter = z // 4, lax.rem(z, 4)

    def tail_copy(slot, which, target):
        return pltpu.make_async_remote_copy(
            src_ref=x_out.at[:, 3, pl.ds(64 - TAIL, TAIL)], dst_ref=tail_out.at[slot],
            send_sem=tail_send.at[which], recv_sem=tail_recv.at[slot],
            device_id=(blk, target, w), device_id_type=MESH,
        )

    @pl.when(quarter != 3)
    def _():
        tail_copy(0, 0, lax.rem(z + 1, 8)).start()

    @pl.when(quarter == 3)
    def _():
        tail_copy(part, 0, 0).start()
        tail_copy(part, 1, 4).start()

    column(sibling, 1, sibling).wait_recv()
    column(sibling_across, 2, sibling).wait_recv()

    @pl.when(quarter != 0)
    def _():
        tail_copy(0, 0, lax.rem(z + 1, 8)).wait_recv()

    @pl.when(quarter == 0)
    def _():
        tail_copy(0, 0, lax.rem(z + 1, 8)).wait_recv()
        tail_copy(1, 0, lax.rem(z + 1, 8)).wait_recv()

    tail_copy(0, 0, lax.rem(z + 1, 8)).wait_send()

    @pl.when(quarter == 3)
    def _():
        tail_copy(0, 1, lax.rem(z + 1, 8)).wait_send()

    def low_sent(k, carry):
        low_copy(k).wait_send()
        return carry

    def x_sent(k, carry):
        x_copy(k).wait_send()
        return carry

    own_kv.wait()

    def kv_done(k, carry):
        source = lax.rem(z + k, 8)
        pltpu.make_async_remote_copy(
            src_ref=kv_out.at[source], dst_ref=kv_out.at[source], send_sem=kv_send.at[0],
            recv_sem=kv_recv.at[source], device_id=(blk, z, w), device_id_type=MESH,
        ).wait_recv()
        kv_copy(k).wait_send()
        return carry

    lax.fori_loop(1, 8, kv_done, 0)

    @pl.when(z != 0)
    def _():
        for slot in range(2):
            across_plane(slot).wait_recv()
            across_plane(slot).wait_send()

    @pl.when(z == 0)
    def _():
        across_here(0).wait()
        across_here(1).wait()

    lax.fori_loop(1, 8, low_sent, 0)
    lax.fori_loop(1, 32, x_sent, 0)
    over.wait_send()
    beside.wait_send()
    relay.wait_send()


def intake_call(x, low, kv, weight, params):
    anywhere = pl.BlockSpec(memory_space=pl.ANY)
    sems = pltpu.SemaphoreType.DMA
    return pl.pallas_call(
        intake_kernel,
        in_specs=[anywhere] * 5,
        out_specs=[anywhere] * 8,
        out_shape=[
            jax.ShapeDtypeStruct((8, 4, 64, COLS), jnp.bfloat16),
            jax.ShapeDtypeStruct((8, 4, 64, WIDE), jnp.bfloat16),
            jax.ShapeDtypeStruct((2, 8, TAIL, COLS), jnp.bfloat16),
            jax.ShapeDtypeStruct((8, 64, 2 * HD), jnp.bfloat16),
            jax.ShapeDtypeStruct(weight.shape, weight.dtype),
            jax.ShapeDtypeStruct(params.shape, params.dtype),
            jax.ShapeDtypeStruct(weight.shape, weight.dtype),
            jax.ShapeDtypeStruct(params.shape, params.dtype),
        ],
        scratch_shapes=[
            sems((3,)), sems((8,)), sems((8,)), sems((4,)), sems((4,)), sems((32,)), sems((32,)), sems((8,)), sems((8,)),
            sems((3,)), sems((3,)),
            sems((2,)), sems((2,)),
        ],
        compiler_params=pltpu.CompilerParams(collective_id=0, has_side_effects=True),
        name="intake",
    )(x, low, kv, weight, params)


def states_kernel(
    order_ref, end_ref, sum_ref, rate_ref, start_ref,
    got_end, got_sum, chain, reply, own_sem, end_send, end_recv, sum_send, sum_recv, back_send, back_recv,
):
    blk, z, w = lax.axis_index("blk"), lax.axis_index("z"), lax.axis_index("w")
    barrier = pltpu.get_barrier_semaphore()

    def greet(k, carry):
        pl.semaphore_signal(barrier, inc=1, device_id=(blk, lax.rem(z + k, 8), w), device_id_type=MESH)
        return carry

    lax.fori_loop(1, 8, greet, 0)
    pl.semaphore_wait(barrier, 7)
    mine = pl.ds(pl.multiple_of(z * 8, 8), 8)

    def remote(src, dst, send, recv, target):
        return pltpu.make_async_remote_copy(
            src_ref=src, dst_ref=dst, send_sem=send, recv_sem=recv, device_id=(blk, target, w), device_id_type=MESH
        )

    def end_copy(k):
        peer = lax.rem(z + k, 8)
        return remote(
            end_ref.at[peer // 2, :, lax.rem(peer, 2)], got_end.at[mine], end_send.at[k], end_recv.at[z], peer
        )

    def sum_copy(k):
        peer = lax.rem(z + k, 8)
        return remote(sum_ref.at[peer // 2], got_sum.at[mine], sum_send.at[k], sum_recv.at[z], peer)

    def back_copy(k):
        peer = lax.rem(z + k, 8)
        return remote(
            reply.at[pl.ds(pl.multiple_of(peer * 8, 8), 8)], start_ref.at[z // 2, :, lax.rem(z, 2)],
            back_send.at[k], back_recv.at[z], peer,
        )

    def send_ends(k, carry):
        end_copy(k).start()
        sum_copy(k).start()
        return carry

    lax.fori_loop(1, 8, send_ends, 0)
    own_end = pltpu.make_async_copy(end_ref.at[z // 2, :, lax.rem(z, 2)], got_end.at[mine], own_sem.at[0])
    own_sum = pltpu.make_async_copy(sum_ref.at[z // 2], got_sum.at[mine], own_sem.at[1])
    own_end.start()
    own_sum.start()
    own_end.wait()
    own_sum.wait()

    def ends_arrived(k, carry):
        source = lax.rem(z + k, 8)
        there = pl.ds(pl.multiple_of(source * 8, 8), 8)
        remote(got_end.at[there], got_end.at[there], end_send.at[0], end_recv.at[source], z).wait_recv()
        remote(got_sum.at[there], got_sum.at[there], sum_send.at[0], sum_recv.at[source], z).wait_recv()
        return carry

    lax.fori_loop(1, 8, ends_arrived, 0)
    rate = rate_ref[z // 2, lax.rem(z, 2)]

    def carry_on(position, state):
        chain[position] = state
        index = order_ref[position]
        return jnp.exp2(rate * got_sum[pl.ds(index, 1), :]) * state + got_end[index]

    lax.fori_loop(0, 64, carry_on, jnp.zeros((8, 128), jnp.float32))

    def pick(index, carry):
        reply[index] = chain[order_ref[64 + index]]
        return carry

    lax.fori_loop(0, 64, pick, 0)

    def send_back(k, carry):
        back_copy(k).start()
        return carry

    lax.fori_loop(1, 8, send_back, 0)
    own_back = pltpu.make_async_copy(reply.at[mine], start_ref.at[z // 2, :, lax.rem(z, 2)], own_sem.at[2])
    own_back.start()
    own_back.wait()

    def finish(k, carry):
        source = lax.rem(z + k, 8)
        landed = start_ref.at[source // 2, :, lax.rem(source, 2)]
        remote(landed, landed, back_send.at[0], back_recv.at[source], z).wait_recv()
        end_copy(k).wait_send()
        sum_copy(k).wait_send()
        back_copy(k).wait_send()
        return carry

    lax.fori_loop(1, 8, finish, 0)


def states_call(order, ends, sums, rate):
    f32 = jnp.float32
    here = pl.BlockSpec(memory_space=pltpu.VMEM)
    sems = pltpu.SemaphoreType.DMA
    return pl.pallas_call(
        states_kernel,
        in_specs=[pl.BlockSpec(memory_space=pltpu.SMEM), here, here, here],
        out_specs=here,
        out_shape=jax.ShapeDtypeStruct((TILES, CHUNKS, 2, 8, 128), f32),
        scratch_shapes=[
            pltpu.VMEM((64, 8, 128), f32), pltpu.VMEM((64, 128), f32), pltpu.VMEM((64, 8, 128), f32),
            pltpu.VMEM((64, 8, 128), f32), sems((3,)), sems((8,)), sems((8,)), sems((8,)), sems((8,)),
            sems((8,)), sems((8,)),
        ],
        compiler_params=pltpu.CompilerParams(collective_id=1, has_side_effects=True),
        name="chain_states",
    )(order, ends, sums, rate)


ULYS = ("z", "w")
PLANE = ("blk", "w")


def local(
    mamba_input, gate_input, delta_low, state_mixers, conv_weight, conv_bias, delta_weight, delta_bias,
    decay_log, skip_gain, queries, key_rows, value_rows, span_order,
):
    f32 = jnp.float32
    me, z = lax.axis_index("blk"), lax.axis_index("z")
    zpart = z // 4
    params = jnp.concatenate(
        [
            -jnp.exp(decay_log) * LOG2E, conv_weight.astype(f32), conv_bias[None, :], delta_bias[None, :],
            skip_gain[None, :], jnp.zeros((1, COLS), f32),
        ],
        axis=0,
    )
    places = jnp.arange(16, dtype=jnp.int32)
    mine = lax.dynamic_slice_in_dim(span_order, 2 * me, 2, 0)

    low_mix = jnp.concatenate(
        [delta_low, state_mixers, jnp.zeros((64, WIDE - 512 - 2 * STATE), jnp.bfloat16)], axis=1
    )
    kv = jnp.concatenate([key_rows.reshape(64, 8, HD), value_rows.reshape(64, 8, HD)], axis=2)
    x, low_mix, tails, kv, weight, params, _, _ = intake_call(
        mamba_input, low_mix, kv.reshape(64, 8 * 2 * HD), delta_weight, params
    )
    x, gate_input, queries = lax.optimization_barrier((x, gate_input, queries))
    rate = params[:STATE]
    low = low_mix.reshape(CHUNKS, CLEN, WIDE)
    mix = (
        low[:, :, 512 : 512 + 2 * STATE].swapaxes(0, 1).reshape(CHUNKS * CLEN, 2 * STATE)
    )
    x = x.reshape(CHUNKS, CLEN, COLS)
    places = places[:, None]
    earlier = span_order.reshape(CHUNKS, 2)[:, zpart] - 1
    follows = (earlier[:, None] == span_order[None, :]).astype(jnp.bfloat16)
    at_start = lax.rem(z, 4) == 0
    tails = tails[:, :, TAIL - 8 :]
    of_block = tails.swapaxes(0, 1).reshape(16, 8, COLS)
    before = jnp.einsum("cj,jtk->ctk", follows, of_block, preferred_element_type=f32)
    prior = jnp.where(at_start, before, tails[0].astype(f32))
    spread = jnp.repeat(jnp.eye(2 * STATE, dtype=jnp.bfloat16), 128, axis=1)

    y, cum, end, sums = scan_call(
        x, prior, low, mix, spread, weight, params[16:20], params[20:21], params[21:22], rate, params[22:23],
    )

    gate = lax.all_to_all(gate_input, PLANE, split_axis=1, concat_axis=0, tiled=True)
    query = lax.all_to_all(queries, ULYS, split_axis=1, concat_axis=0, tiled=True)
    kv = lax.all_gather(kv.reshape(512, 2 * HD), PLANE, axis=0, tiled=True).reshape(8, 4, 2, 256, 2 * HD)

    items = jnp.arange(17, dtype=jnp.int32)
    second = (items > mine[0]).astype(jnp.int32)
    place = jnp.where(second == 1, items - mine[0] - 1, items)
    stored = jnp.sum(jnp.where(place[:, None] == span_order[None, :], places.T, 0), axis=1)
    diag = (place == jnp.where(second == 1, mine[1], mine[0])).astype(jnp.int32)
    first = (place == 0).astype(jnp.int32)
    attended = attention_call(
        second, stored // 2, stored % 2, diag, first, query.reshape(2, SPAN, HD), kv
    ).reshape(2 * SPAN, HD)

    steps = jnp.arange(64, dtype=jnp.int32)
    at = jnp.sum(jnp.where((steps // 4)[:, None] == span_order[None, :], places.T, 0), axis=1)
    index_of = ((at % 2) * 4 + steps % 4) * 8 + at // 2
    block_of = 2 * (steps % 8) + steps // 32
    place_of = jnp.sum(jnp.where(block_of[:, None] == places.T, span_order[None, :], 0), axis=1)
    position_of = place_of * 4 + (steps // 8) % 4
    starts = states_call(
        jnp.concatenate([index_of, position_of]), end.reshape(TILES, CHUNKS, 2, 8, 128), sums,
        rate.reshape(2, 8, TILES, 128).transpose(2, 0, 1, 3),
    )
    gated = finish_call(
        y, cum, mix[:, STATE:], spread[:STATE, : STATE * 128], gate.reshape(CHUNKS, CLEN, COLS), rate,
        starts.reshape(TILES, CHUNKS * STATE, 128),
    ).reshape(CHUNKS * CLEN, COLS)
    mamba_output = lax.all_to_all(gated, PLANE, split_axis=0, concat_axis=1, tiled=True)
    attention_output = lax.all_to_all(attended, ULYS, split_axis=0, concat_axis=1, tiled=True)
    return (mamba_output, attention_output)


def solution(mesh):
    tokens = P(("blk", "z", "w"), None)
    wide = P(None, ULYS)
    flat = P(ULYS)
    placed = (
        tokens, tokens, tokens, tokens, wide, flat, wide, flat, wide, flat, tokens, tokens, tokens, P(),
    )
    split_mesh = Mesh(mesh.devices.reshape(8, 8, 4), ("blk", "z", "w"))
    return jax.shard_map(
        local, mesh=split_mesh, in_specs=placed, out_specs=(tokens, tokens), check_vma=False
    )
```
